128 devices in a mesh: batch: 8 (over x, core), tensor: 16 (over y, z).
Axes of the slice: x: 4, y: 4, z: 4, core: 2. Of those that a mesh axis runs over, the one named last changes fastest.
Arguments:
- tokens: bfloat16 [256, 8192], P('batch'), may hold values from -6 to 6
- row_adapter_index: int32 [256], P('batch'), may hold values from 0 to 31, as said below
- adapter_store_row: int32 [32], replicated, may hold values from 0 to 31, as said below
- lengths: int32 [256], P('batch'), may hold values from 2 to 512, as said below
- query_weight: bfloat16 [8192, 8192], P(None, 'tensor'), may hold values from -0.0625 to 0.0625
- key_weight: bfloat16 [8192, 1024], P(None, 'tensor'), may hold values from -0.0625 to 0.0625
- value_weight: bfloat16 [8192, 1024], P(None, 'tensor'), may hold values from -0.0625 to 0.0625
- output_weight: bfloat16 [8192, 8192], P('tensor'), may hold values from -0.09375 to 0.09375
- adapter_down_weight: bfloat16 [32, 48, 8192], P('batch', None, 'tensor'), may hold values from -0.0625 to 0.0625
- adapter_up_query: bfloat16 [32, 16, 8192], P('batch', None, 'tensor'), may hold values from -1.5 to 1.5
- adapter_up_key: bfloat16 [32, 16, 1024], P('batch', None, 'tensor'), may hold values from -1.5 to 1.5
- adapter_up_value: bfloat16 [32, 16, 1024], P('batch', None, 'tensor'), may hold values from -1.5 to 1.5
- cached_key_rows: bfloat16 [256, 512, 1024], P(('batch', 'tensor')), may hold values from -530 to 530
- cached_value_rows: bfloat16 [256, 512, 1024], P(('batch', 'tensor')), may hold values from -6 to 6
Outputs:
- attn_out: bfloat16 [256, 8192], P('batch', 'tensor')
The draws below stay inside these ranges and needn't reach their ends.
Inputs may be any that keep to these rules, and one draw needn't show every extreme that they name: A permutation: adapter a lies in row adapter_store_row[a] of the adapter arrays; rows o * 4 to (o + 1) * 4 - 1 lie with batch group o. `row_adapter_index`: of the rows of one batch group, at most 8 have adapters stored with any one batch group, and exactly 8 with some batch group. `lengths`: the first row of each batch group has all 512 positions.
All inputs are finite; a program needn't handle non-finite values.
Results may differ from the reference program's by a relative error of at most 0.035.
Values may be sent and summed in bfloat16 or wider, within the bound.
A program may use at most 64 MiB of HBM per device.

```python
import math
import jax
import jax.numpy as jnp
from jax import lax

MODEL_WIDTH = 8192
QUERY_HEADS = 64
KEY_VALUE_HEADS = 8
HEAD_WIDTH = 128
ADAPTER_RANK = 16
ADAPT_DEV = 4
ROWS_DEV = 32
CACHE = 512
ROWS = 256
ADAPTER_COUNT = 32
CAP = 8


def slot_table(key):
    return jax.random.permutation(key, ADAPTER_COUNT).astype(jnp.int32)


def draw_adapter_store_row(key, part):
    return slot_table(key)


def draw_row_adapter_index(key, part):
    table = slot_table(key)
    key = jax.random.fold_in(key, 1)
    groups = ADAPTER_COUNT // ADAPT_DEV
    owners_all = (jnp.arange(groups * CAP, dtype=jnp.int32) // CAP).astype(jnp.int32)
    inverse = jnp.zeros((ADAPTER_COUNT,), jnp.int32).at[table].set(jnp.arange(ADAPTER_COUNT, dtype=jnp.int32))

    def one_block(block_key):
        key_one, key_two, key_three, key_four = jax.random.split(block_key, 4)
        full_owner = jax.random.randint(key_one, (), 0, groups)
        ranking = jax.random.permutation(key_two, groups * CAP).astype(jnp.int32)
        ranking = jnp.where(owners_all == full_owner, -1 - jnp.arange(groups * CAP, dtype=jnp.int32), ranking)
        ordering = jnp.argsort(ranking)
        chosen = owners_all[ordering[:ROWS_DEV]]
        chosen = jax.random.permutation(key_three, chosen)
        within = jax.random.randint(key_four, (ROWS_DEV,), 0, ADAPT_DEV)
        return inverse[chosen * ADAPT_DEV + within]
    block_keys = jax.random.split(key, ROWS // ROWS_DEV)
    return jax.vmap(one_block)(block_keys).reshape(ROWS).astype(jnp.int32)


def draw_lengths(key, part):
    key = jax.random.fold_in(key, 2)
    values = jax.random.randint(key, (ROWS,), 2, CACHE + 1)
    first_rows = jnp.arange(ROWS) % ROWS_DEV == 0
    return jnp.where(first_rows, CACHE, values).astype(jnp.int32)


def draw_cached_key_rows(key, part):
    key = jax.random.fold_in(key, 3)
    key_one = jax.random.fold_in(key, 0)
    values = jax.random.normal(key_one, (ROWS, CACHE, KEY_VALUE_HEADS * HEAD_WIDTH), jnp.float32)
    return jnp.clip(values, -4.5, 4.5).astype(jnp.bfloat16)


def with_spikes(array, stream_key, source, target, blocks, factor):
    owner, partner = [(jnp.arange(array.shape[dim]) // (array.shape[dim] // blocks)).reshape([-1 if axis == dim else 1 for axis in range(array.ndim)]) for dim in (source, target)]
    chosen = jax.random.permutation(stream_key, blocks)[partner]
    strong = (owner == chosen) | (owner == (partner + blocks // 2) % blocks)
    return jnp.where(strong, factor * array, array)


def steps_of(key, dims, cuts, low, largest):
    loudness = 1.0
    for position, blocks in cuts:
        steps = jax.random.uniform(jax.random.fold_in(jax.random.fold_in(key, 6), position), (blocks,), jnp.float32, low / len(cuts), largest / len(cuts))
        loudness = loudness * jnp.repeat(jnp.exp(steps), dims[position] // blocks).reshape((-1,) + (1,) * (len(dims) - 1 - position))
    return loudness


def centred(key, shape, width, limit, cuts=(), kind=jnp.bfloat16):
    array = jax.random.normal(key, shape, jnp.float32) * width
    if len(cuts) > 0:
        array = steps_of(key, shape, cuts, -0.22, 0.18) * array
    return jnp.clip(array, min=-limit, max=limit).astype(kind)


def bell_draw_with(rng, extent, deviation, reach, shards, heavy, kind=jnp.bfloat16):
    drawn = deviation * jax.random.normal(rng, extent, jnp.float32)
    if shards:
        drawn = drawn * steps_of(rng, extent, shards, -0.22, 0.18)
    return jnp.clip(with_spikes(drawn, jax.random.fold_in(rng, 3), *heavy), -reach, reach).astype(kind)


def setup_inputs(seed: int = 0) -> dict:
    key_of = jax.random.split(jax.random.key(seed), 15)
    tokens = centred(key_of[0], (ROWS, MODEL_WIDTH), 1.0, 6.0, ((0, 8),))
    row_adapter_index = draw_row_adapter_index(jax.random.fold_in(key_of[14], 71), 0)
    adapter_store_row = draw_adapter_store_row(jax.random.fold_in(key_of[14], 71), 0)
    lengths = draw_lengths(jax.random.fold_in(key_of[14], 71), 0)
    query_weight = centred(key_of[4], (MODEL_WIDTH, QUERY_HEADS * HEAD_WIDTH), MODEL_WIDTH ** -0.5, 0.0625, ((1, 16),))
    key_weight = centred(key_of[5], (MODEL_WIDTH, KEY_VALUE_HEADS * HEAD_WIDTH), MODEL_WIDTH ** -0.5, 0.0625, ((1, 16),))
    value_weight = centred(key_of[6], (MODEL_WIDTH, KEY_VALUE_HEADS * HEAD_WIDTH), MODEL_WIDTH ** -0.5, 0.0625, ((1, 16),))
    output_weight = bell_draw_with(key_of[7], (QUERY_HEADS * HEAD_WIDTH, MODEL_WIDTH), (QUERY_HEADS * HEAD_WIDTH) ** -0.5, 0.09375, ((0, 16),), (0, 1, 16, 2.0))
    adapter_down_weight = centred(key_of[8], (ADAPTER_COUNT, 3 * ADAPTER_RANK, MODEL_WIDTH), MODEL_WIDTH ** -0.5, 0.0625, ((0, 8), (2, 16)))
    adapter_up_query = centred(key_of[9], (ADAPTER_COUNT, ADAPTER_RANK, QUERY_HEADS * HEAD_WIDTH), ADAPTER_RANK ** -0.5, 1.5, ((0, 8), (2, 16)))
    adapter_up_key = centred(key_of[10], (ADAPTER_COUNT, ADAPTER_RANK, KEY_VALUE_HEADS * HEAD_WIDTH), ADAPTER_RANK ** -0.5, 1.5, ((0, 8), (2, 16)))
    adapter_up_value = centred(key_of[11], (ADAPTER_COUNT, ADAPTER_RANK, KEY_VALUE_HEADS * HEAD_WIDTH), ADAPTER_RANK ** -0.5, 1.5, ((0, 8), (2, 16)))
    cached_key_rows = draw_cached_key_rows(jax.random.fold_in(key_of[14], 71), 0)
    cached_value_rows = centred(key_of[13], (ROWS, CACHE, KEY_VALUE_HEADS * HEAD_WIDTH), 1.0, 6.0, ((0, 128),))
    return {"tokens": tokens, "row_adapter_index": row_adapter_index, "adapter_store_row": adapter_store_row, "lengths": lengths, "query_weight": query_weight, "key_weight": key_weight, "value_weight": value_weight, "output_weight": output_weight, "adapter_down_weight": adapter_down_weight, "adapter_up_query": adapter_up_query, "adapter_up_key": adapter_up_key, "adapter_up_value": adapter_up_value, "cached_key_rows": cached_key_rows, "cached_value_rows": cached_value_rows}


ADAPTER_SCALE = 0.5

def reference(tokens, row_adapter_index, adapter_store_row, lengths, query_weight, key_weight, value_weight, output_weight, adapter_down_weight, adapter_up_query, adapter_up_key, adapter_up_value, cached_key_rows, cached_value_rows):
    row_count = tokens.shape[0]
    store_ids = jnp.arange(ADAPTER_COUNT, dtype=jnp.int32)
    slot_rows = lax.optimization_barrier(jnp.sum(jnp.where(row_adapter_index[:, None] == store_ids[None, :], adapter_store_row[None, :], 0), axis=1)).astype(jnp.int32)
    select = slot_rows[:, None] == store_ids[None, :]
    adapter_terms = jnp.dot(tokens, adapter_down_weight.reshape(ADAPTER_COUNT * 3 * ADAPTER_RANK, MODEL_WIDTH).T, preferred_element_type=jnp.float32)
    adapter_terms = adapter_terms.reshape(row_count, ADAPTER_COUNT, 3 * ADAPTER_RANK)
    down_projected = lax.optimization_barrier(jnp.sum(jnp.where(select[:, :, None], adapter_terms, 0.0), axis=1))
    scaled_terms = (ADAPTER_SCALE * down_projected).astype(jnp.bfloat16)
    deltas = []
    for projection_choice, up_weight_table in enumerate((adapter_up_query, adapter_up_key, adapter_up_value)):
        piece_cols = scaled_terms[:, projection_choice * ADAPTER_RANK:(projection_choice + 1) * ADAPTER_RANK]
        masked = jnp.where(select[:, :, None], piece_cols[:, None, :], jnp.zeros((), jnp.bfloat16))
        masked = masked.reshape(row_count, ADAPTER_COUNT * ADAPTER_RANK)
        product = jnp.dot(masked, up_weight_table.reshape(ADAPTER_COUNT * ADAPTER_RANK, up_weight_table.shape[2]), preferred_element_type=jnp.float32)
        deltas.append(product.astype(jnp.bfloat16))
    queries = (jnp.dot(tokens, query_weight, preferred_element_type=jnp.float32) + deltas[0].astype(jnp.float32)).astype(jnp.bfloat16)
    keys_new = (jnp.dot(tokens, key_weight, preferred_element_type=jnp.float32) + deltas[1].astype(jnp.float32)).astype(jnp.bfloat16)
    values_new = (jnp.dot(tokens, value_weight, preferred_element_type=jnp.float32) + deltas[2].astype(jnp.float32)).astype(jnp.bfloat16)
    head_group = QUERY_HEADS // KEY_VALUE_HEADS
    score_scale = 1.0 / math.sqrt(HEAD_WIDTH)

    def one_row(items):
        query_row, key_row, value_row, cached_keys, cached_values, length = items
        query_heads = query_row.reshape(KEY_VALUE_HEADS, head_group, HEAD_WIDTH).astype(jnp.float32)
        cached_keys = cached_keys.reshape(CACHE, KEY_VALUE_HEADS, HEAD_WIDTH).astype(jnp.float32)
        cached_values = cached_values.reshape(CACHE, KEY_VALUE_HEADS, HEAD_WIDTH).astype(jnp.float32)
        scores = jnp.einsum('ghd,pgd->ghp', query_heads, cached_keys) * score_scale
        self_score = jnp.einsum('ghd,gd->gh', query_heads, key_row.reshape(KEY_VALUE_HEADS, HEAD_WIDTH).astype(jnp.float32)) * score_scale
        is_valid = (jnp.arange(CACHE, dtype=jnp.int32) < length)[None, None, :]
        top_score = jnp.maximum(lax.optimization_barrier(jnp.max(jnp.where(is_valid, scores, -jnp.inf), axis=2)), self_score)
        weights = jnp.where(is_valid, jnp.exp(scores - top_score[..., None]), 0.0)
        self_weight = jnp.exp(self_score - top_score)
        full_total = lax.optimization_barrier(jnp.sum(weights, axis=2)) + self_weight
        rounded = lax.optimization_barrier(weights.astype(jnp.bfloat16)).astype(jnp.float32)
        rounded_self = lax.optimization_barrier(self_weight.astype(jnp.bfloat16)).astype(jnp.float32)
        numerator = jnp.einsum('ghp,pgd->ghd', rounded, cached_values)
        numerator = numerator + rounded_self[..., None] * value_row.reshape(KEY_VALUE_HEADS, 1, HEAD_WIDTH).astype(jnp.float32)
        return (numerator / full_total[..., None]).astype(jnp.bfloat16).reshape(QUERY_HEADS * HEAD_WIDTH)
    attended = lax.map(one_row, (queries, keys_new, values_new, cached_key_rows, cached_value_rows, lengths))
    return jnp.dot(attended, output_weight, preferred_element_type=jnp.float32).astype(jnp.bfloat16)
```

```python
import functools
import math

import jax
import jax.numpy as jnp
from jax import lax
from jax.experimental import pallas as pl
from jax.experimental.pallas import tpu as pltpu
from jax.sharding import PartitionSpec as P

HEAD_WIDTH = 128
ADAPTER_SCALE = 0.5
MASKED_SCORE = -1e30
MESH = pl.DeviceIdType.MESH
F32 = jnp.float32
BF16 = jnp.bfloat16

GROUPS = 8
SPLIT = 16
CAP = 8
ROWS = 32
QUERY_CHUNKS = 8
DEPTH = 8192
COLS = 512
SPAN = 512
TRANS_B = (((1,), (1,)), ((), ()))


def iota(shape, dim):
    return lax.broadcasted_iota(jnp.int32, shape, dim)


def dot(a, b):
    return jnp.dot(a, b, preferred_element_type=F32)


def dot_tb(a, b):
    return lax.dot_general(a, b, TRANS_B, preferred_element_type=F32)


def kernel(
    index_ref,
    store_ref,
    length_ref,
    tokens_hbm,
    query_hbm,
    key_hbm,
    value_hbm,
    output_hbm,
    down_hbm,
    up_query_hbm,
    up_key_hbm,
    up_value_hbm,
    cache_key_hbm,
    cache_value_hbm,
    out_ref,
    tokens,
    query_w,
    kv_w,
    output_w,
    down,
    up_query,
    up_key,
    up_value,
    cache_key,
    cache_value,
    send1,
    recv1,
    send2,
    recv2,
    send3,
    recv3,
    stage_q,
    stage_kv,
    send4,
    recv4,
    send5,
    recv5,
    send6,
    recv6,
    local_sem,
    query_sem,
    ssem1,
    rsem1,
    ssem2,
    rsem2,
    ssem3,
    rsem3,
    ssem4,
    rsem4,
    ssem5,
    rsem5,
    ssem6,
    rsem6,
):
    me_b = lax.axis_index("batch")
    me_t = lax.axis_index("tensor")

    def fetch(src, dst, sem):
        copy = pltpu.make_async_copy(src, dst, sem)
        copy.start()
        return copy

    get_tokens = fetch(tokens_hbm, tokens, local_sem.at[0])
    get_down = fetch(down_hbm, down.at[:, pl.ds(0, 48), :], local_sem.at[1])
    get_up = [
        fetch(up_query_hbm, up_query, local_sem.at[2]),
        fetch(up_key_hbm, up_key, local_sem.at[3]),
        fetch(up_value_hbm, up_value, local_sem.at[4]),
    ]
    get_kv = [
        fetch(key_hbm, kv_w.at[pl.ds(0, 64), :], local_sem.at[5]),
        fetch(value_hbm, kv_w.at[pl.ds(64, 64), :], local_sem.at[6]),
    ]
    piece = DEPTH // QUERY_CHUNKS
    get_query = [
        fetch(
            query_hbm.at[pl.ds(i * piece, piece), :],
            query_w.at[pl.ds(i * piece, piece), :],
            query_sem.at[i],
        )
        for i in range(QUERY_CHUNKS)
    ]
    get_key = fetch(cache_key_hbm, cache_key, local_sem.at[7])
    get_value = fetch(cache_value_hbm, cache_value, local_sem.at[8])
    get_output = [
        fetch(
            output_hbm.at[pl.ds(i * 128, 128), :],
            output_w.at[pl.ds(i * 128, 128), :],
            local_sem.at[9 + i],
        )
        for i in range(4)
    ]

    barrier = pltpu.get_barrier_semaphore()

    def greet_b(i, carry):
        peer = lax.rem(me_b + i, GROUPS)
        pl.semaphore_signal(barrier, inc=1, device_id={"batch": peer}, device_id_type=MESH)
        return carry

    def greet_t(i, carry):
        peer = lax.rem(me_t + i, SPLIT)
        pl.semaphore_signal(barrier, inc=1, device_id={"tensor": peer}, device_id_type=MESH)
        return carry

    lax.fori_loop(1, GROUPS, greet_b, 0)
    lax.fori_loop(1, SPLIT, greet_t, 0)

    down[:, pl.ds(48, 80), :] = jnp.zeros((4, 80, COLS), BF16)

    row_i = iota((ROWS, ROWS), 0)
    col_i = iota((ROWS, ROWS), 1)
    diag = row_i == col_i
    index_c = jnp.broadcast_to(index_ref[...].astype(F32), (ROWS, ROWS))
    store_c = jnp.broadcast_to(store_ref[...].astype(F32), (ROWS, ROWS))
    index_r = jnp.sum(jnp.where(diag, index_c, 0.0), axis=1, keepdims=True)
    slot_r = jnp.sum(
        jnp.where(index_r == col_i.astype(F32), store_c, 0.0), axis=1, keepdims=True
    )
    slot_c = jnp.sum(jnp.where(diag, slot_r, 0.0), axis=0, keepdims=True)
    owner_r = jnp.floor(slot_r * 0.25)
    owner_c = jnp.floor(slot_c * 0.25)
    within_r = slot_r - 4.0 * owner_r
    place_c = jnp.sum(
        jnp.where((owner_r == owner_c) & (row_i < col_i), 1.0, 0.0), axis=0, keepdims=True
    )
    target_c = owner_c * CAP + place_c
    slots = GROUPS * CAP
    route = jnp.where(target_c == iota((slots, ROWS), 0).astype(F32), 1.0, 0.0).astype(BF16)
    hot = jnp.where(within_r == iota((ROWS, 128), 1).astype(F32), 1.0, 0.0).astype(BF16)

    get_tokens.wait()
    own = tokens[:, pl.ds(pl.multiple_of(me_t * COLS, COLS), COLS)]
    routed = dot(route, own).reshape(GROUPS, CAP, COLS)
    routed_hot = dot(route, hot).reshape(GROUPS, CAP, 128)
    send1[:, :, 0:256] = jnp.concatenate(
        [routed[:, :, 0:256], routed[:, :, 256:512]], axis=1
    ).astype(BF16)
    send1[:, :, 256:384] = jnp.concatenate(
        [routed_hot, jnp.zeros_like(routed_hot)], axis=1
    ).astype(BF16)

    pl.semaphore_wait(barrier, GROUPS - 1 + SPLIT - 1)

    def start_all(axis, me, count, source, target, ssem, rsem):
        def body(i, carry):
            peer = lax.rem(me + i, count)
            pltpu.make_async_remote_copy(
                src_ref=source(peer),
                dst_ref=target.at[me],
                send_sem=ssem.at[peer],
                recv_sem=rsem.at[me],
                device_id={axis: peer},
                device_id_type=MESH,
            ).start()
            return carry

        lax.fori_loop(1, count, body, 0)

    def wait_all(axis, me, count, source, target, ssem, rsem, which):
        def body(i, carry):
            peer = lax.rem(me + i, count)
            copy = pltpu.make_async_remote_copy(
                src_ref=source(peer),
                dst_ref=target.at[peer],
                send_sem=ssem.at[peer],
                recv_sem=rsem.at[peer],
                device_id={axis: peer},
                device_id_type=MESH,
            )
            if which == "recv":
                copy.wait_recv()
            else:
                copy.wait_send()
            return carry

        lax.fori_loop(1, count, body, 0)

    phase1 = ("batch", me_b, GROUPS, lambda p: send1.at[p], recv1, ssem1, rsem1)
    start_all(*phase1)
    recv1[me_b] = send1[me_b]

    for copy in get_kv:
        copy.wait()
    kv_base = dot_tb(tokens[...], kv_w[...])

    def query_part(total, chunks):
        for i in chunks:
            get_query[i].wait()
            total = total + dot(
                tokens[:, i * piece : (i + 1) * piece], query_w[i * piece : (i + 1) * piece, :]
            )
        return total

    q_base = jnp.zeros((ROWS, COLS), F32)

    wait_all(*phase1, "recv")
    got = recv1[...].astype(F32)
    rows_in = jnp.concatenate([got[:, 0:8, 0:256], got[:, 8:16, 0:256]], axis=2).reshape(
        slots, COLS
    )
    hot_in = got[:, 0:8, 256:384].reshape(slots, 128)
    get_down.wait()
    shrunk = jnp.zeros((slots, 128), F32)
    for a in range(4):
        shrunk = shrunk + dot_tb((rows_in * hot_in[:, a : a + 1]).astype(BF16), down[a])
    send2[...] = (shrunk[0:32] + pltpu.roll(shrunk[32:64], 64, 1)).astype(BF16)

    phase2 = ("tensor", me_t, SPLIT, lambda p: send2, recv2, ssem2, rsem2)
    start_all(*phase2)
    recv2[me_t] = send2[...]

    q_base = query_part(q_base, range(0, 4))

    wait_all(*phase2, "recv")
    summed = jnp.sum(recv2[...].astype(F32), axis=0)
    scaled = (ADAPTER_SCALE * summed).astype(BF16)
    lane_in = iota((128, 256), 0)
    lane_out = iota((128, 256), 1)
    wanted = (lane_out // 64) * 16 + lane_out % 16
    pick_lo = jnp.where((lane_in == wanted) & (lane_out < 192), 1.0, 0.0).astype(BF16)
    pick_hi = jnp.where((lane_in == wanted + 64) & (lane_out < 192), 1.0, 0.0).astype(BF16)
    spread_hot = jnp.where(lane_in == (lane_out % 64) // 16, 1.0, 0.0).astype(BF16)
    spread = jnp.concatenate([dot(scaled, pick_lo), dot(scaled, pick_hi)], axis=0)
    masked = (spread * dot(hot_in.astype(BF16), spread_hot)).astype(BF16)
    for copy in get_up:
        copy.wait()
    delta_q = dot(masked[:, 0:64], up_query[...].reshape(64, COLS))
    delta_k = dot(masked[:, 64:128], up_key[...].reshape(64, 64))
    delta_v = dot(masked[:, 128:192], up_value[...].reshape(64, 64))
    delta_kv = jnp.concatenate([delta_k, delta_v], axis=1)
    delta_q = delta_q.reshape(GROUPS, CAP, COLS)
    delta_kv = delta_kv.reshape(GROUPS, CAP, 128)
    send3[:, :, 0:256] = jnp.concatenate(
        [delta_q[:, :, 0:256], delta_q[:, :, 256:512]], axis=1
    ).astype(BF16)
    send3[:, :, 256:384] = jnp.concatenate(
        [delta_kv, jnp.zeros_like(delta_kv)], axis=1
    ).astype(BF16)

    phase3 = ("batch", me_b, GROUPS, lambda p: send3.at[p], recv3, ssem3, rsem3)
    start_all(*phase3)
    recv3[me_b] = send3[me_b]

    q_base = query_part(q_base, range(4, QUERY_CHUNKS))

    wait_all(*phase3, "recv")
    back = recv3[...].astype(F32)
    back = jnp.concatenate(
        [back[:, 0:8, 0:256], back[:, 8:16, 0:256], back[:, 0:8, 256:384]], axis=2
    ).reshape(slots, COLS + 128)
    delta = lax.dot_general(
        route, back.astype(BF16), (((0,), (0,)), ((), ())), preferred_element_type=F32
    )
    q_new = q_base + delta[:, 0:COLS]
    kv_new = kv_base + delta[:, COLS:]
    parity = lax.rem(me_t, 2)
    rolled = pltpu.roll(kv_new, 64, 1)
    half = iota((ROWS, 128), 1) // 64 == parity
    k_row = jnp.where(half, jnp.where(parity == 1, rolled, kv_new), 0.0)
    v_row = jnp.where(half, jnp.where(parity == 1, kv_new, rolled), 0.0)
    stage_kv[...] = jnp.zeros_like(stage_kv)
    for j in range(4):
        stage_q[pl.ds(j, ROWS, stride=4), :] = q_new[:, 128 * j : 128 * (j + 1)]
    stage_kv[pl.ds(0, ROWS, stride=4), :] = k_row
    stage_kv[pl.ds(1, ROWS, stride=4), :] = v_row
    send4[...] = jnp.concatenate(
        [stage_q[...].reshape(SPLIT, 8, 128), stage_kv[...].reshape(SPLIT, 8, 128)], axis=1
    ).astype(BF16)

    phase4 = ("tensor", me_t, SPLIT, lambda p: send4.at[p], recv4, ssem4, rsem4)
    start_all(*phase4)
    recv4[me_t] = send4[me_t]

    lane = iota((1, 128), 1)
    lane_row = (lane % 8) // 4
    length_lane = iota((1, ROWS), 1)
    lengths = length_ref[...].astype(F32)
    length0 = jnp.sum(jnp.where(length_lane == 2 * me_t, lengths, 0.0), axis=1, keepdims=True)
    length1 = jnp.sum(jnp.where(length_lane == 2 * me_t + 1, lengths, 0.0), axis=1, keepdims=True)
    limit = jnp.where(lane_row == 0, length0, length1)

    wait_all(*phase4, "recv")
    arrived = recv4[...].astype(F32)
    q_all = arrived[:, 0:8, :].reshape(128, 128)
    kv_all = jnp.sum(arrived[:, 8:16, :].reshape(8, 2, 8, 128), axis=1)
    tail = jnp.concatenate([kv_all[g] for g in range(8)], axis=1)
    head_row = iota((128, 128), 0) // 16
    blocks = jnp.concatenate(
        [jnp.where(head_row == g, q_all, 0.0).astype(BF16) for g in range(8)], axis=1
    )
    get_key.wait()
    scores = jnp.where(
        lane_row == 0, dot_tb(cache_key[0], blocks), dot_tb(cache_key[1], blocks)
    )
    self_scores = dot_tb(tail.astype(BF16), blocks)
    score_scale = 1.0 / math.sqrt(HEAD_WIDTH)
    valid = iota((SPAN, 128), 0).astype(F32) < limit
    scores = jnp.where(valid, scores * score_scale, MASKED_SCORE)
    self_valid = iota((8, 128), 0) == 4 * lane_row
    self_scores = jnp.where(self_valid, self_scores * score_scale, MASKED_SCORE)
    top = jnp.maximum(
        jnp.max(scores, axis=0, keepdims=True), jnp.max(self_scores, axis=0, keepdims=True)
    )
    weights = jnp.exp(scores - top)
    self_weight = jnp.exp(self_scores - top)
    full_total = jnp.sum(weights, axis=0, keepdims=True) + jnp.sum(
        self_weight, axis=0, keepdims=True
    )
    weights_t = jnp.transpose(weights).astype(BF16)
    extra_t = jnp.transpose(
        jnp.concatenate(
            [self_weight, jnp.broadcast_to(full_total, (8, 128)), jnp.zeros((112, 128), F32)],
            axis=0,
        )
    )
    self_t = extra_t[:, 0:8].astype(BF16)
    total_t = extra_t[:, 8:9]
    tail_v = pltpu.roll(tail, 7, 0).astype(BF16)
    get_value.wait()
    row_of = (iota((32, 128), 0) % 8) // 4
    attended = []
    for pair in range(4):
        part = weights_t[32 * pair : 32 * (pair + 1), :]
        cols = slice(256 * pair, 256 * (pair + 1))
        over = [dot(part, cache_value[r, :, cols]) for r in range(2)]
        last = dot(self_t[32 * pair : 32 * (pair + 1), :], tail_v[:, cols])
        both = [o + last for o in over]
        mine = [jnp.concatenate([o[0:16, 0:128], o[16:32, 128:256]], axis=0) for o in both]
        attended.append(jnp.where(row_of == 0, mine[0], mine[1]))
    send5[...] = (jnp.concatenate(attended, axis=0) / total_t).reshape(SPLIT, 8, 128)

    phase5 = ("tensor", me_t, SPLIT, lambda p: send5.at[p], recv5, ssem5, rsem5)
    start_all(*phase5)
    recv5[me_t] = send5[me_t]
    for copy in get_output:
        copy.wait()
    wait_all(*phase5, "recv")
    stage_q[...] = recv5[...].reshape(128, 128)
    heads = jnp.concatenate(
        [stage_q[pl.ds(j, ROWS, stride=4), :].astype(BF16) for j in range(4)], axis=1
    )

    def project(i, carry):
        peer = lax.rem(me_t + i, SPLIT)
        cols = pl.ds(pl.multiple_of(peer * COLS, COLS), COLS)
        send6[peer] = dot(heads, output_w[:, cols]).astype(BF16)
        pltpu.make_async_remote_copy(
            src_ref=send6.at[peer],
            dst_ref=recv6.at[me_t],
            send_sem=ssem6.at[peer],
            recv_sem=rsem6.at[me_t],
            device_id={"tensor": peer},
            device_id_type=MESH,
        ).start()
        return carry

    lax.fori_loop(1, SPLIT, project, 0)
    own_cols = pl.ds(pl.multiple_of(me_t * COLS, COLS), COLS)
    total = dot(heads, output_w[:, own_cols])

    phase6 = ("tensor", me_t, SPLIT, lambda p: send6.at[p], recv6, ssem6, rsem6)
    wait_all(*phase6, "recv")

    def add_up(i, total):
        return total + recv6[lax.rem(me_t + i, SPLIT)].astype(F32)

    total = lax.fori_loop(1, SPLIT, add_up, total)
    out_ref[...] = total.astype(BF16)

    for phase in (phase1, phase2, phase3, phase4, phase5, phase6):
        wait_all(*phase, "send")


def on_device(
    tokens,
    row_adapter_index,
    adapter_store_row,
    lengths,
    query_weight,
    key_weight,
    value_weight,
    output_weight,
    adapter_down_weight,
    adapter_up_query,
    adapter_up_key,
    adapter_up_value,
    cached_key_rows,
    cached_value_rows,
):
    small = pl.BlockSpec(memory_space=pltpu.VMEM)
    large = pl.BlockSpec(memory_space=pltpu.HBM)
    dma = pltpu.SemaphoreType.DMA
    return pl.pallas_call(
        kernel,
        out_shape=jax.ShapeDtypeStruct((ROWS, COLS), BF16),
        in_specs=[small] * 3 + [large] * 11,
        out_specs=small,
        scratch_shapes=[
            pltpu.VMEM((ROWS, DEPTH), BF16),
            pltpu.VMEM((DEPTH, COLS), BF16),
            pltpu.VMEM((128, DEPTH), BF16),
            pltpu.VMEM((COLS, DEPTH), BF16),
            pltpu.VMEM((4, 128, COLS), BF16),
            pltpu.VMEM((4, 16, COLS), BF16),
            pltpu.VMEM((4, 16, 64), BF16),
            pltpu.VMEM((4, 16, 64), BF16),
            pltpu.VMEM((2, SPAN, 1024), BF16),
            pltpu.VMEM((2, SPAN, 1024), BF16),
            pltpu.VMEM((GROUPS, 16, 384), BF16),
            pltpu.VMEM((GROUPS, 16, 384), BF16),
            pltpu.VMEM((32, 128), BF16),
            pltpu.VMEM((SPLIT, 32, 128), BF16),
            pltpu.VMEM((GROUPS, 16, 384), BF16),
            pltpu.VMEM((GROUPS, 16, 384), BF16),
            pltpu.VMEM((128, 128), F32),
            pltpu.VMEM((128, 128), F32),
            pltpu.VMEM((SPLIT, 16, 128), BF16),
            pltpu.VMEM((SPLIT, 16, 128), BF16),
            pltpu.VMEM((SPLIT, 8, 128), F32),
            pltpu.VMEM((SPLIT, 8, 128), F32),
            pltpu.VMEM((SPLIT, ROWS, COLS), BF16),
            pltpu.VMEM((SPLIT, ROWS, COLS), BF16),
            dma((13,)),
            dma((QUERY_CHUNKS,)),
            dma((GROUPS,)),
            dma((GROUPS,)),
            dma((SPLIT,)),
            dma((SPLIT,)),
            dma((GROUPS,)),
            dma((GROUPS,)),
            dma((SPLIT,)),
            dma((SPLIT,)),
            dma((SPLIT,)),
            dma((SPLIT,)),
            dma((SPLIT,)),
            dma((SPLIT,)),
        ],
        compiler_params=pltpu.CompilerParams(
            collective_id=0, has_side_effects=True, vmem_limit_bytes=56 * 1024 * 1024
        ),
    )(
        row_adapter_index.reshape(1, ROWS),
        adapter_store_row.reshape(1, 32),
        lengths.reshape(1, ROWS),
        tokens,
        query_weight,
        key_weight.T,
        value_weight.T,
        output_weight,
        adapter_down_weight,
        adapter_up_query,
        adapter_up_key,
        adapter_up_value,
        cached_key_rows,
        cached_value_rows,
    )


def solution(mesh):
    placed = (
        P("batch", None),
        P("batch"),
        P(),
        P("batch"),
        P(None, "tensor"),
        P(None, "tensor"),
        P(None, "tensor"),
        P("tensor", None),
        P("batch", None, "tensor"),
        P("batch", None, "tensor"),
        P("batch", None, "tensor"),
        P("batch", None, "tensor"),
        P(("batch", "tensor"), None, None),
        P(("batch", "tensor"), None, None),
    )
    return jax.shard_map(
        on_device, mesh=mesh, in_specs=placed, out_specs=P("batch", "tensor"), check_vma=False
    )
```

```python
import math

import jax
import jax.numpy as jnp
from jax import lax
from jax.experimental import pallas as pl
from jax.experimental.pallas import tpu as pltpu
from jax.sharding import PartitionSpec as P

HEAD_WIDTH = 128
ADAPTER_SCALE = 0.5
MASKED_SCORE = -1e30
MESH = pl.DeviceIdType.MESH
F32 = jnp.float32
BF16 = jnp.bfloat16

GROUPS = 8
SPLIT = 16
CAP = 8
ROWS = 32
QUERY_CHUNKS = 8
DEPTH = 8192
COLS = 512
SPAN = 512
TRANS_B = (((1,), (1,)), ((), ()))


def iota(shape, dim):
    return lax.broadcasted_iota(jnp.int32, shape, dim)


def dot(a, b):
    return jnp.dot(a, b, preferred_element_type=F32)


def dot_tb(a, b):
    return lax.dot_general(a, b, TRANS_B, preferred_element_type=F32)


def far_first(count):
    steps = [(dy, dz) for dy in range(4) for dz in range(4) if dy or dz]
    return sorted(steps, key=lambda s: -(min(s[0], 4 - s[0]) + min(s[1], 4 - s[1])))


TENSOR_STEPS = far_first(SPLIT)
BATCH_STEPS = [(2, 1), (2, 0), (1, 1), (3, 1), (1, 0), (3, 0), (0, 1)]


def kernel(
    index_hbm,
    store_hbm,
    length_hbm,
    tokens_hbm,
    query_hbm,
    key_hbm,
    value_hbm,
    output_hbm,
    down_hbm,
    up_query_hbm,
    up_key_hbm,
    up_value_hbm,
    cache_key_hbm,
    cache_value_hbm,
    out_ref,
    index_ref,
    store_ref,
    length_ref,
    own_tokens,
    tokens,
    query_w,
    kv_w,
    output_w,
    down,
    up_query,
    up_key,
    up_value,
    cache_key,
    cache_value,
    send1,
    recv1,
    send2,
    recv2,
    send3,
    recv3,
    stage_q,
    stage_kv,
    send4,
    recv4,
    send5,
    recv5,
    send6,
    recv6,
    local_sem,
    query_sem,
    send_sem,
    rsem1,
    rsem2,
    rsem3,
    rsem4,
    rsem5,
    rsem6,
):
    me_b = lax.axis_index("batch")
    me_t = lax.axis_index("tensor")
    me_x, me_c = me_b // 2, lax.rem(me_b, 2)
    me_y, me_z = me_t // 4, lax.rem(me_t, 4)

    def batch_peer(step):
        core = 1 - me_c if step[1] else me_c
        return lax.rem(me_x + step[0], 4) * 2 + core

    def tensor_peer(step):
        return lax.rem(me_y + step[0], 4) * 4 + lax.rem(me_z + step[1], 4)

    batch_peers = [batch_peer(step) for step in BATCH_STEPS]
    tensor_peers = [tensor_peer(step) for step in TENSOR_STEPS]

    barrier = pltpu.get_barrier_semaphore()
    for peer in tensor_peers:
        pl.semaphore_signal(barrier, inc=1, device_id={"tensor": peer}, device_id_type=MESH)
    for peer in batch_peers:
        pl.semaphore_signal(barrier, inc=1, device_id={"batch": peer}, device_id_type=MESH)

    pending = []

    def fetch(src, dst, sem):
        copy = pltpu.make_async_copy(src, dst, sem)
        copy.start()
        pending.append(copy)
        return copy

    def need(*copies):
        for copy in copies:
            if any(copy is other for other in pending):
                pending[:] = [other for other in pending if other is not copy]
                copy.wait()

    own_cols = pl.ds(pl.multiple_of(me_t * COLS, COLS), COLS)
    get_index = fetch(index_hbm, index_ref, local_sem.at[0])
    get_store = fetch(store_hbm, store_ref, local_sem.at[1])
    get_own = fetch(tokens_hbm.at[:, own_cols], own_tokens, local_sem.at[2])
    get_down = [
        fetch(down_hbm.at[a], down.at[pl.ds(64 * a, 48), :], local_sem.at[3 + a]) for a in range(4)
    ]
    get_up = [
        fetch(up_query_hbm, up_query, local_sem.at[7]),
        fetch(up_key_hbm, up_key, local_sem.at[8]),
        fetch(up_value_hbm, up_value, local_sem.at[9]),
    ]
    get_length = fetch(length_hbm, length_ref, local_sem.at[10])
    get_tokens = fetch(tokens_hbm, tokens, local_sem.at[11])
    get_kv = [
        fetch(key_hbm, kv_w.at[pl.ds(0, 64), :], local_sem.at[12]),
        fetch(value_hbm, kv_w.at[pl.ds(64, 64), :], local_sem.at[13]),
    ]
    piece = DEPTH // QUERY_CHUNKS
    get_query = [
        fetch(
            query_hbm.at[pl.ds(i * piece, piece), :],
            query_w.at[pl.ds(i * piece, piece), :],
            query_sem.at[i],
        )
        for i in range(QUERY_CHUNKS)
    ]
    get_key = fetch(cache_key_hbm, cache_key, local_sem.at[14])
    get_value = fetch(cache_value_hbm, cache_value, local_sem.at[15])
    get_output = [
        fetch(
            output_hbm.at[pl.ds(i * 128, 128), :],
            output_w.at[pl.ds(i * 128, 128), :],
            local_sem.at[16 + i],
        )
        for i in range(4)
    ]

    row_i = iota((ROWS, ROWS), 0)
    col_i = iota((ROWS, ROWS), 1)
    diag = row_i == col_i
    need(get_index, get_store)
    index_c = jnp.broadcast_to(index_ref[...].astype(F32), (ROWS, ROWS))
    store_c = jnp.broadcast_to(store_ref[...].astype(F32), (ROWS, ROWS))
    index_r = jnp.sum(jnp.where(diag, index_c, 0.0), axis=1, keepdims=True)
    slot_r = jnp.sum(
        jnp.where(index_r == col_i.astype(F32), store_c, 0.0), axis=1, keepdims=True
    )
    slot_c = jnp.sum(jnp.where(diag, slot_r, 0.0), axis=0, keepdims=True)
    owner_r = jnp.floor(slot_r * 0.25)
    owner_c = jnp.floor(slot_c * 0.25)
    within_r = slot_r - 4.0 * owner_r
    same = owner_r == owner_c
    place_c = jnp.sum(jnp.where(same & (row_i < col_i), 1.0, 0.0), axis=0, keepdims=True)
    target_c = owner_c * 16.0 + place_c
    slot_i = iota((128, ROWS), 0)
    route = jnp.where(
        target_c == ((slot_i // 16) * 16 + slot_i % 8).astype(F32), 1.0, 0.0
    ).astype(BF16)
    hot = jnp.where(within_r == iota((ROWS, 128), 1).astype(F32), 1.0, 0.0).astype(BF16)
    lower = (iota((128, 256), 0) % 16) < 8

    need(get_own)
    routed = dot(route, own_tokens[...])
    routed_hot = dot(route, hot)
    send1[:, :, 0:256] = (
        jnp.where(lower, routed[:, 0:256], routed[:, 256:512]).astype(BF16).reshape(GROUPS, 16, 256)
    )
    send1[:, :, 256:384] = routed_hot.astype(BF16).reshape(GROUPS, 16, 128)

    pl.semaphore_wait(barrier, GROUPS - 1 + SPLIT - 1)

    def remote(axis, peer, source, target, phase, rsem):
        return pltpu.make_async_remote_copy(
            src_ref=source,
            dst_ref=target,
            send_sem=send_sem.at[phase],
            recv_sem=rsem,
            device_id={axis: peer},
            device_id_type=MESH,
        )

    def start_batch(phase, send, recv, rsem):
        for peer in batch_peers:
            remote("batch", peer, send.at[peer], recv.at[me_b], phase, rsem.at[me_b]).start()

    def wait_batch(phase, send, recv, rsem):
        for peer in batch_peers[::-1]:
            remote("batch", peer, send.at[peer], recv.at[peer], phase, rsem.at[peer]).wait_recv()

    def sent(phase, like):
        pltpu.make_async_copy(like, like, send_sem.at[phase]).wait()

    start_batch(0, send1, recv1, rsem1)
    recv1[me_b] = send1[me_b]

    for a in range(4):
        down[pl.ds(64 * a + 48, 16), :] = jnp.zeros((16, COLS), BF16)
    place_r = jnp.sum(jnp.where(same & (col_i < row_i), 1.0, 0.0), axis=1, keepdims=True)
    target_r = owner_r * 16.0 + place_r
    slot_j = iota((ROWS, 128), 1).astype(F32)
    unroute = jnp.concatenate(
        [
            jnp.where(target_r == slot_j, 1.0, 0.0),
            jnp.where(target_r + 8.0 == slot_j, 1.0, 0.0),
        ],
        axis=0,
    ).astype(BF16)
    lane_in = iota((128, 256), 0)
    lane_out = iota((128, 256), 1)
    group_hot = jnp.where(lane_in == lane_out // 64, 1.0, 0.0).astype(BF16)
    turn = jnp.where(lane_out < 64, 16, jnp.where(lane_out < 128, 32, 0))
    wanted = jnp.where(lane_out < 192, turn + lane_out % 16, -256)
    pick = jnp.concatenate(
        [jnp.where(lane_in == wanted, 1.0, 0.0), jnp.where(lane_in == wanted + 64, 1.0, 0.0)],
        axis=1,
    ).astype(BF16)
    spread_hot = jnp.where(lane_in == (lane_out % 64) // 16, 1.0, 0.0).astype(BF16)

    need(get_tokens, *get_kv)
    kv_base = dot_tb(tokens[...], kv_w[...])

    def query_part(total, chunks):
        for i in chunks:
            need(get_query[i])
            total = total + dot(
                tokens[:, i * piece : (i + 1) * piece], query_w[i * piece : (i + 1) * piece, :]
            )
        return total

    q_base = query_part(jnp.zeros((ROWS, COLS), F32), range(0, 3))
    need(*get_down)

    wait_batch(0, send1, recv1, rsem1)
    rows_in = recv1[:, :, 0:256].reshape(128, 256)
    hot_in = recv1[:, :, 256:384].reshape(128, 128)
    empty = jnp.zeros_like(rows_in)
    rows_in = jnp.concatenate(
        [jnp.where(lower, rows_in, empty), jnp.where(lower, empty, rows_in)], axis=1
    )
    shrunk = dot_tb(rows_in, down[...]) * dot(hot_in, group_hot)
    shrunk = shrunk[:, 0:128] + shrunk[:, 128:256]
    shrunk = jnp.sum(shrunk.reshape(GROUPS, 2, CAP, 128), axis=1).reshape(64, 128)
    shrunk = shrunk + pltpu.roll(shrunk, 64, 1)
    send2[...] = jnp.where(iota((32, 128), 1) < 64, shrunk[0:32], shrunk[32:64]).astype(BF16)

    for peer in tensor_peers:
        remote("tensor", peer, send2, recv2.at[me_t], 1, rsem2.at[me_t]).start()

    hot_rows = dot(hot_in, spread_hot).reshape(GROUPS, 2, CAP, 256)[:, 0].reshape(64, 256)
    need(*get_up)
    up_k = up_key[...].reshape(64, 64)
    up_v = up_value[...].reshape(64, 64)
    blank = jnp.zeros_like(up_k)
    up_kv = jnp.concatenate(
        [jnp.concatenate([up_k, blank], axis=1), jnp.concatenate([blank, up_v], axis=1)], axis=0
    )
    q_base = query_part(q_base, range(3, QUERY_CHUNKS))

    summed = send2[...].astype(F32)
    for peer in tensor_peers[::-1]:
        remote("tensor", peer, send2, recv2.at[peer], 1, rsem2.at[peer]).wait_recv()
        summed = summed + recv2[peer].astype(F32)
    scaled = (ADAPTER_SCALE * summed).astype(BF16)
    spread = dot(scaled, pick)
    spread = jnp.concatenate([spread[:, 0:256], spread[:, 256:512]], axis=0)
    masked = (spread * hot_rows).astype(BF16)
    delta_kv = dot(masked[:, 0:128], up_kv).reshape(GROUPS, CAP, 128)
    delta_q = dot(masked[:, 128:192], up_query[...].reshape(64, COLS)).reshape(GROUPS, CAP, COLS)
    send3[:, :, 0:256] = jnp.concatenate(
        [delta_q[:, :, 0:256], delta_q[:, :, 256:512]], axis=1
    ).astype(BF16)
    send3[:, :, 256:384] = jnp.concatenate([delta_kv, delta_kv], axis=1).astype(BF16)

    start_batch(2, send3, recv3, rsem3)
    recv3[me_b] = send3[me_b]

    parity = lax.rem(me_t, 2)
    half = iota((ROWS, 128), 1) // 64 == parity
    stage_kv[...] = jnp.zeros_like(stage_kv)
    need(get_length)
    lane = iota((1, 128), 1)
    lane_row = (lane % 8) // 4
    length_lane = iota((1, ROWS), 1)
    lengths = length_ref[...].astype(F32)
    length0 = jnp.sum(jnp.where(length_lane == 2 * me_t, lengths, 0.0), axis=1, keepdims=True)
    length1 = jnp.sum(jnp.where(length_lane == 2 * me_t + 1, lengths, 0.0), axis=1, keepdims=True)
    limit = jnp.where(lane_row == 0, length0, length1)

    wait_batch(2, send3, recv3, rsem3)
    delta = dot(unroute, recv3[...].reshape(128, 384))
    kv_new = kv_base + delta[0:32, 256:384]
    rolled = pltpu.roll(kv_new, 64, 1)
    k_row = jnp.where(half, jnp.where(parity == 1, rolled, kv_new), 0.0)
    v_row = jnp.where(half, jnp.where(parity == 1, kv_new, rolled), 0.0)
    for j in range(4):
        part = delta[32 * (j // 2) : 32 * (j // 2) + 32, 128 * (j % 2) : 128 * (j % 2) + 128]
        stage_q[pl.ds(j, ROWS, stride=4), :] = q_base[:, 128 * j : 128 * (j + 1)] + part
    stage_kv[pl.ds(0, ROWS, stride=4), :] = k_row
    stage_kv[pl.ds(1, ROWS, stride=4), :] = v_row
    send4[...] = jnp.concatenate(
        [stage_q[...].reshape(SPLIT, 8, 128), stage_kv[...].reshape(SPLIT, 8, 128)], axis=1
    ).astype(BF16)

    for peer in tensor_peers:
        remote("tensor", peer, send4.at[peer], recv4.at[me_t], 3, rsem4.at[me_t]).start()
    recv4[me_t] = send4[me_t]
    need(get_key, get_value, *get_output)
    score_scale = 1.0 / math.sqrt(HEAD_WIDTH)
    valid = iota((SPAN, 128), 0).astype(F32) < limit
    self_valid = iota((8, 128), 0) == 4 * lane_row
    head_row = iota((128, 128), 0) // 16
    row_of = (iota((32, 128), 0) % 8) // 4

    for peer in tensor_peers[::-1]:
        remote("tensor", peer, send4.at[peer], recv4.at[peer], 3, rsem4.at[peer]).wait_recv()
    arrived = recv4[...].astype(F32)
    q_all = arrived[:, 0:8, :].reshape(128, 128)
    kv_all = jnp.sum(arrived[:, 8:16, :].reshape(8, 2, 8, 128), axis=1)
    tail = jnp.concatenate([kv_all[g] for g in range(8)], axis=1)
    blocks = jnp.concatenate(
        [jnp.where(head_row == g, q_all, 0.0).astype(BF16) for g in range(8)], axis=1
    )
    scores = jnp.where(
        lane_row == 0, dot_tb(cache_key[0], blocks), dot_tb(cache_key[1], blocks)
    )
    self_scores = dot_tb(tail.astype(BF16), blocks)
    scores = jnp.where(valid, scores * score_scale, MASKED_SCORE)
    self_scores = jnp.where(self_valid, self_scores * score_scale, MASKED_SCORE)
    top = jnp.maximum(
        jnp.max(scores, axis=0, keepdims=True), jnp.max(self_scores, axis=0, keepdims=True)
    )
    weights = jnp.exp(scores - top)
    self_weight = jnp.exp(self_scores - top)
    full_total = jnp.sum(weights, axis=0, keepdims=True) + jnp.sum(
        self_weight, axis=0, keepdims=True
    )
    weights_t = jnp.transpose(weights).astype(BF16)
    extra_t = jnp.transpose(
        jnp.concatenate(
            [self_weight, jnp.broadcast_to(full_total, (8, 128)), jnp.zeros((112, 128), F32)],
            axis=0,
        )
    )
    self_t = extra_t[:, 0:8].astype(BF16)
    total_t = extra_t[:, 8:9]
    tail_v = pltpu.roll(tail, 7, 0).astype(BF16)
    attended = []
    for pair in range(4):
        part = weights_t[32 * pair : 32 * (pair + 1), :]
        cols = slice(256 * pair, 256 * (pair + 1))
        over = [dot(part, cache_value[r, :, cols]) for r in range(2)]
        last = dot(self_t[32 * pair : 32 * (pair + 1), :], tail_v[:, cols])
        both = [o + last for o in over]
        mine = [jnp.concatenate([o[0:16, 0:128], o[16:32, 128:256]], axis=0) for o in both]
        attended.append(jnp.where(row_of == 0, mine[0], mine[1]))
    send5[...] = jnp.concatenate(attended, axis=0) / total_t

    def eight(t):
        return pl.ds(pl.multiple_of(8 * t, 8), 8)

    for peer in tensor_peers:
        remote(
            "tensor", peer, send5.at[eight(peer)], recv5.at[eight(me_t)], 4, rsem5.at[me_t]
        ).start()
    recv5[eight(me_t), :] = send5[eight(me_t), :]
    sent(0, send1.at[pl.ds(0, GROUPS - 1)])
    sent(1, recv2.at[pl.ds(0, SPLIT - 1)])
    sent(2, send3.at[pl.ds(0, GROUPS - 1)])
    sent(3, send4.at[pl.ds(0, SPLIT - 1)])
    for peer in tensor_peers[::-1]:
        remote(
            "tensor", peer, send5.at[eight(peer)], recv5.at[eight(peer)], 4, rsem5.at[peer]
        ).wait_recv()
    heads = jnp.concatenate(
        [recv5[pl.ds(j, ROWS, stride=4), :].astype(BF16) for j in range(4)], axis=1
    )

    for peer in tensor_peers:
        cols = pl.ds(pl.multiple_of(peer * COLS, COLS), COLS)
        send6[peer] = dot(heads, output_w[:, cols]).astype(BF16)
        remote("tensor", peer, send6.at[peer], recv6.at[me_t], 5, rsem6.at[me_t]).start()
    total = dot(heads, output_w[:, own_cols])
    for dy, dz in TENSOR_STEPS:
        peer = tensor_peer((4 - dy, 4 - dz))
        remote("tensor", peer, send6.at[peer], recv6.at[peer], 5, rsem6.at[peer]).wait_recv()
        total = total + recv6[peer].astype(F32)
    out_ref[...] = total.astype(BF16)
    sent(4, send5.at[pl.ds(0, 8 * (SPLIT - 1))])
    sent(5, send6.at[pl.ds(0, SPLIT - 1)])


def on_device(
    tokens,
    row_adapter_index,
    adapter_store_row,
    lengths,
    query_weight,
    key_weight,
    value_weight,
    output_weight,
    adapter_down_weight,
    adapter_up_query,
    adapter_up_key,
    adapter_up_value,
    cached_key_rows,
    cached_value_rows,
):
    large = pl.BlockSpec(memory_space=pltpu.HBM)
    dma = pltpu.SemaphoreType.DMA
    return pl.pallas_call(
        kernel,
        out_shape=jax.ShapeDtypeStruct((ROWS, COLS), BF16),
        in_specs=[large] * 14,
        out_specs=pl.BlockSpec(memory_space=pltpu.VMEM),
        scratch_shapes=[
            pltpu.VMEM((1, ROWS), jnp.int32),
            pltpu.VMEM((1, 32), jnp.int32),
            pltpu.VMEM((1, ROWS), jnp.int32),
            pltpu.VMEM((ROWS, COLS), BF16),
            pltpu.VMEM((ROWS, DEPTH), BF16),
            pltpu.VMEM((DEPTH, COLS), BF16),
            pltpu.VMEM((128, DEPTH), BF16),
            pltpu.VMEM((COLS, DEPTH), BF16),
            pltpu.VMEM((256, COLS), BF16),
            pltpu.VMEM((4, 16, COLS), BF16),
            pltpu.VMEM((4, 16, 64), BF16),
            pltpu.VMEM((4, 16, 64), BF16),
            pltpu.VMEM((2, SPAN, 1024), BF16),
            pltpu.VMEM((2, SPAN, 1024), BF16),
            pltpu.VMEM((GROUPS, 16, 384), BF16),
            pltpu.VMEM((GROUPS, 16, 384), BF16),
            pltpu.VMEM((32, 128), BF16),
            pltpu.VMEM((SPLIT, 32, 128), BF16),
            pltpu.VMEM((GROUPS, 16, 384), BF16),
            pltpu.VMEM((GROUPS, 16, 384), BF16),
            pltpu.VMEM((128, 128), F32),
            pltpu.VMEM((128, 128), F32),
            pltpu.VMEM((SPLIT, 16, 128), BF16),
            pltpu.VMEM((SPLIT, 16, 128), BF16),
            pltpu.VMEM((128, 128), F32),
            pltpu.VMEM((128, 128), F32),
            pltpu.VMEM((SPLIT, ROWS, COLS), BF16),
            pltpu.VMEM((SPLIT, ROWS, COLS), BF16),
            dma((20,)),
            dma((QUERY_CHUNKS,)),
            dma((6,)),
            dma((GROUPS,)),
            dma((SPLIT,)),
            dma((GROUPS,)),
            dma((SPLIT,)),
            dma((SPLIT,)),
            dma((SPLIT,)),
        ],
        compiler_params=pltpu.CompilerParams(
            collective_id=0, has_side_effects=True, vmem_limit_bytes=56 * 1024 * 1024
        ),
    )(
        row_adapter_index.reshape(1, ROWS),
        adapter_store_row.reshape(1, 32),
        lengths.reshape(1, ROWS),
        tokens,
        query_weight,
        key_weight.T,
        value_weight.T,
        output_weight,
        adapter_down_weight,
        adapter_up_query,
        adapter_up_key,
        adapter_up_value,
        cached_key_rows,
        cached_value_rows,
    )


def solution(mesh):
    placed = (
        P("batch", None),
        P("batch"),
        P(),
        P("batch"),
        P(None, "tensor"),
        P(None, "tensor"),
        P(None, "tensor"),
        P("tensor", None),
        P("batch", None, "tensor"),
        P("batch", None, "tensor"),
        P("batch", None, "tensor"),
        P("batch", None, "tensor"),
        P(("batch", "tensor"), None, None),
        P(("batch", "tensor"), None, None),
    )
    return jax.shard_map(
        on_device, mesh=mesh, in_specs=placed, out_specs=P("batch", "tensor"), check_vma=False
    )
```

```python
import math

import jax
import jax.numpy as jnp
from jax import lax
from jax.experimental import pallas as pl
from jax.experimental.pallas import tpu as pltpu
from jax.sharding import PartitionSpec as P

HEAD_WIDTH = 128
ADAPTER_SCALE = 0.5
MASKED_SCORE = -1e30
MESH = pl.DeviceIdType.MESH
F32 = jnp.float32
BF16 = jnp.bfloat16

GROUPS = 8
SPLIT = 16
CAP = 8
ROWS = 32
QUERY_CHUNKS = 8
DEPTH = 8192
COLS = 512
SPAN = 512
TRANS_B = (((1,), (1,)), ((), ()))


def iota(shape, dim):
    return lax.broadcasted_iota(jnp.int32, shape, dim)


def dot(a, b):
    return jnp.dot(a, b, preferred_element_type=F32)


def dot_tb(a, b):
    return lax.dot_general(a, b, TRANS_B, preferred_element_type=F32)


def far_first(count):
    steps = [(dy, dz) for dy in range(4) for dz in range(4) if dy or dz]
    return sorted(steps, key=lambda s: -(min(s[0], 4 - s[0]) + min(s[1], 4 - s[1])))


TENSOR_STEPS = far_first(SPLIT)
PLANE_STEPS = (0, 1, 3, 2)
BATCH_STEPS = [(2, 1), (2, 0), (1, 1), (3, 1), (1, 0), (3, 0), (0, 1)]


def kernel(
    index_hbm,
    store_hbm,
    length_hbm,
    tokens_hbm,
    query_hbm,
    key_hbm,
    value_hbm,
    output_hbm,
    down_hbm,
    up_query_hbm,
    up_key_hbm,
    up_value_hbm,
    cache_key_hbm,
    cache_value_hbm,
    out_ref,
    index_ref,
    store_ref,
    length_ref,
    own_tokens,
    tokens,
    query_w,
    kv_w,
    output_w,
    down,
    up_query,
    up_key,
    up_value,
    cache_key,
    cache_value,
    send1,
    recv1,
    send2,
    recv2,
    send3,
    recv3,
    stage_q,
    stage_kv,
    send4,
    recv4,
    send5,
    recv5,
    send6,
    recv6,
    local_sem,
    query_sem,
    send_sem,
    rsem1,
    rsem2,
    rsem3,
    rsem4,
    rsem5,
    rsem6,
):
    me_b = lax.axis_index("batch")
    me_t = lax.axis_index("tensor")
    me_x, me_c = me_b // 2, lax.rem(me_b, 2)
    me_y, me_z = me_t // 4, lax.rem(me_t, 4)

    def batch_peer(step):
        core = 1 - me_c if step[1] else me_c
        return lax.rem(me_x + step[0], 4) * 2 + core

    def tensor_peer(step):
        return lax.rem(me_y + step[0], 4) * 4 + lax.rem(me_z + step[1], 4)

    batch_peers = [batch_peer(step) for step in BATCH_STEPS]
    tensor_peers = [tensor_peer(step) for step in TENSOR_STEPS]

    barrier = pltpu.get_barrier_semaphore()
    for peer in tensor_peers:
        pl.semaphore_signal(barrier, inc=1, device_id={"tensor": peer}, device_id_type=MESH)
    for peer in batch_peers:
        pl.semaphore_signal(barrier, inc=1, device_id={"batch": peer}, device_id_type=MESH)

    pending = []

    def fetch(src, dst, sem):
        copy = pltpu.make_async_copy(src, dst, sem)
        copy.start()
        pending.append(copy)
        return copy

    def need(*copies):
        for copy in copies:
            if any(copy is other for other in pending):
                pending[:] = [other for other in pending if other is not copy]
                copy.wait()

    own_cols = pl.ds(pl.multiple_of(me_t * COLS, COLS), COLS)
    get_index = fetch(index_hbm, index_ref, local_sem.at[0])
    get_store = fetch(store_hbm, store_ref, local_sem.at[1])
    get_own = fetch(tokens_hbm.at[:, own_cols], own_tokens, local_sem.at[2])
    get_down = [
        fetch(down_hbm.at[a], down.at[pl.ds(64 * a, 48), :], local_sem.at[3 + a]) for a in range(4)
    ]
    get_up = [
        fetch(up_query_hbm, up_query, local_sem.at[7]),
        fetch(up_key_hbm, up_key, local_sem.at[8]),
        fetch(up_value_hbm, up_value, local_sem.at[9]),
    ]
    get_length = fetch(length_hbm, length_ref, local_sem.at[10])
    get_tokens = fetch(tokens_hbm, tokens, local_sem.at[11])
    get_kv = [
        fetch(key_hbm, kv_w.at[pl.ds(0, 64), :], local_sem.at[12]),
        fetch(value_hbm, kv_w.at[pl.ds(64, 64), :], local_sem.at[13]),
    ]
    piece = DEPTH // QUERY_CHUNKS
    get_query = [
        fetch(
            query_hbm.at[pl.ds(i * piece, piece), :],
            query_w.at[pl.ds(i * piece, piece), :],
            query_sem.at[i],
        )
        for i in range(QUERY_CHUNKS)
    ]
    get_key = fetch(cache_key_hbm, cache_key, local_sem.at[14])
    get_value = fetch(cache_value_hbm, cache_value, local_sem.at[15])
    get_output = [
        fetch(
            output_hbm.at[pl.ds(i * 128, 128), :],
            output_w.at[pl.ds(i * 128, 128), :],
            local_sem.at[16 + i],
        )
        for i in range(4)
    ]

    row_i = iota((ROWS, ROWS), 0)
    col_i = iota((ROWS, ROWS), 1)
    diag = row_i == col_i
    need(get_index, get_store)
    index_c = jnp.broadcast_to(index_ref[...].astype(F32), (ROWS, ROWS))
    store_c = jnp.broadcast_to(store_ref[...].astype(F32), (ROWS, ROWS))
    index_r = jnp.sum(jnp.where(diag, index_c, 0.0), axis=1, keepdims=True)
    slot_r = jnp.sum(
        jnp.where(index_r == col_i.astype(F32), store_c, 0.0), axis=1, keepdims=True
    )
    slot_c = jnp.sum(jnp.where(diag, slot_r, 0.0), axis=0, keepdims=True)
    owner_r = jnp.floor(slot_r * 0.25)
    owner_c = jnp.floor(slot_c * 0.25)
    within_r = slot_r - 4.0 * owner_r
    same = owner_r == owner_c
    place_c = jnp.sum(jnp.where(same & (row_i < col_i), 1.0, 0.0), axis=0, keepdims=True)
    target_c = owner_c * 16.0 + place_c
    slot_i = iota((128, ROWS), 0)
    route = jnp.where(
        target_c == ((slot_i // 16) * 16 + slot_i % 8).astype(F32), 1.0, 0.0
    ).astype(BF16)
    hot = jnp.where(within_r == iota((ROWS, 128), 1).astype(F32), 1.0, 0.0).astype(BF16)
    lower = (iota((128, 256), 0) % 16) < 8

    need(get_own)
    routed = dot(route, own_tokens[...])
    routed_hot = dot(route, hot)
    send1[:, :, 0:256] = (
        jnp.where(lower, routed[:, 0:256], routed[:, 256:512]).astype(BF16).reshape(GROUPS, 16, 256)
    )
    send1[:, :, 256:384] = routed_hot.astype(BF16).reshape(GROUPS, 16, 128)

    pl.semaphore_wait(barrier, GROUPS - 1 + SPLIT - 1)

    def remote(axis, peer, source, target, phase, rsem):
        return pltpu.make_async_remote_copy(
            src_ref=source,
            dst_ref=target,
            send_sem=send_sem.at[phase],
            recv_sem=rsem,
            device_id={axis: peer},
            device_id_type=MESH,
        )

    def start_batch(phase, send, recv, rsem):
        for peer in batch_peers:
            remote("batch", peer, send.at[peer], recv.at[me_b], phase, rsem.at[me_b]).start()

    def wait_batch(phase, send, recv, rsem):
        for peer in batch_peers[::-1]:
            remote("batch", peer, send.at[peer], recv.at[peer], phase, rsem.at[peer]).wait_recv()

    def sent(phase, like):
        pltpu.make_async_copy(like, like, send_sem.at[phase]).wait()

    start_batch(0, send1, recv1, rsem1)
    recv1[me_b] = send1[me_b]

    for a in range(4):
        down[pl.ds(64 * a + 48, 16), :] = jnp.zeros((16, COLS), BF16)
    place_r = jnp.sum(jnp.where(same & (col_i < row_i), 1.0, 0.0), axis=1, keepdims=True)
    target_r = owner_r * 16.0 + place_r
    slot_j = iota((ROWS, 128), 1).astype(F32)
    unroute = jnp.concatenate(
        [
            jnp.where(target_r == slot_j, 1.0, 0.0),
            jnp.where(target_r + 8.0 == slot_j, 1.0, 0.0),
        ],
        axis=0,
    ).astype(BF16)
    lane_in = iota((128, 256), 0)
    lane_out = iota((128, 256), 1)
    group_hot = jnp.where(lane_in == lane_out // 64, 1.0, 0.0).astype(BF16)
    turn = jnp.where(lane_out < 64, 16, jnp.where(lane_out < 128, 32, 0))
    wanted = jnp.where(lane_out < 192, turn + lane_out % 16, -256)
    pick = jnp.concatenate(
        [jnp.where(lane_in == wanted, 1.0, 0.0), jnp.where(lane_in == wanted + 64, 1.0, 0.0)],
        axis=1,
    ).astype(BF16)
    spread_hot = jnp.where(lane_in == (lane_out % 64) // 16, 1.0, 0.0).astype(BF16)

    need(get_tokens, *get_kv)
    kv_base = dot_tb(tokens[...], kv_w[...])

    def query_part(total, chunks):
        for i in chunks:
            need(get_query[i])
            total = total + dot(
                tokens[:, i * piece : (i + 1) * piece], query_w[i * piece : (i + 1) * piece, :]
            )
        return total

    q_base = query_part(jnp.zeros((ROWS, COLS), F32), range(0, 3))
    need(*get_down)

    wait_batch(0, send1, recv1, rsem1)
    rows_in = recv1[:, :, 0:256].reshape(128, 256)
    hot_in = recv1[:, :, 256:384].reshape(128, 128)
    empty = jnp.zeros_like(rows_in)
    rows_in = jnp.concatenate(
        [jnp.where(lower, rows_in, empty), jnp.where(lower, empty, rows_in)], axis=1
    )
    shrunk = dot_tb(rows_in, down[...]) * dot(hot_in, group_hot)
    shrunk = shrunk[:, 0:128] + shrunk[:, 128:256]
    shrunk = jnp.sum(shrunk.reshape(GROUPS, 2, CAP, 128), axis=1).reshape(64, 128)
    shrunk = shrunk + pltpu.roll(shrunk, 64, 1)
    send2[...] = jnp.where(iota((32, 128), 1) < 64, shrunk[0:32], shrunk[32:64]).astype(BF16)

    for peer in tensor_peers:
        remote("tensor", peer, send2, recv2.at[me_t], 1, rsem2.at[me_t]).start()

    hot_rows = dot(hot_in, spread_hot).reshape(GROUPS, 2, CAP, 256)[:, 0].reshape(64, 256)
    need(*get_up)
    up_k = up_key[...].reshape(64, 64)
    up_v = up_value[...].reshape(64, 64)
    blank = jnp.zeros_like(up_k)
    up_kv = jnp.concatenate(
        [jnp.concatenate([up_k, blank], axis=1), jnp.concatenate([blank, up_v], axis=1)], axis=0
    )
    q_base = query_part(q_base, range(3, QUERY_CHUNKS))

    summed = send2[...].astype(F32)
    for peer in tensor_peers[::-1]:
        remote("tensor", peer, send2, recv2.at[peer], 1, rsem2.at[peer]).wait_recv()
        summed = summed + recv2[peer].astype(F32)
    scaled = (ADAPTER_SCALE * summed).astype(BF16)
    spread = dot(scaled, pick)
    spread = jnp.concatenate([spread[:, 0:256], spread[:, 256:512]], axis=0)
    masked = (spread * hot_rows).astype(BF16)
    delta_kv = dot(masked[:, 0:128], up_kv).reshape(GROUPS, CAP, 128)
    delta_q = dot(masked[:, 128:192], up_query[...].reshape(64, COLS)).reshape(GROUPS, CAP, COLS)
    send3[:, :, 0:256] = jnp.concatenate(
        [delta_q[:, :, 0:256], delta_q[:, :, 256:512]], axis=1
    ).astype(BF16)
    send3[:, :, 256:384] = jnp.concatenate([delta_kv, delta_kv], axis=1).astype(BF16)

    start_batch(2, send3, recv3, rsem3)
    recv3[me_b] = send3[me_b]

    parity = lax.rem(me_t, 2)
    half = iota((ROWS, 128), 1) // 64 == parity
    stage_kv[...] = jnp.zeros_like(stage_kv)
    need(get_length)
    length_lane = iota((1, ROWS), 1)
    lengths = length_ref[...].astype(F32)
    length0 = jnp.sum(jnp.where(length_lane == 2 * me_t, lengths, 0.0), axis=1, keepdims=True)
    length1 = jnp.sum(jnp.where(length_lane == 2 * me_t + 1, lengths, 0.0), axis=1, keepdims=True)

    wait_batch(2, send3, recv3, rsem3)
    delta = dot(unroute, recv3[...].reshape(128, 384))
    kv_new = kv_base + delta[0:32, 256:384]
    rolled = pltpu.roll(kv_new, 64, 1)
    k_row = jnp.where(half, jnp.where(parity == 1, rolled, kv_new), 0.0)
    v_row = jnp.where(half, jnp.where(parity == 1, kv_new, rolled), 0.0)
    for j in range(4):
        part = delta[32 * (j // 2) : 32 * (j // 2) + 32, 128 * (j % 2) : 128 * (j % 2) + 128]
        stage_q[pl.ds(j, ROWS, stride=4), :] = q_base[:, 128 * j : 128 * (j + 1)] + part
    stage_kv[pl.ds(0, ROWS, stride=4), :] = k_row
    stage_kv[pl.ds(1, ROWS, stride=4), :] = v_row
    send4[...] = jnp.concatenate(
        [stage_q[...].reshape(SPLIT, 8, 128), stage_kv[...].reshape(SPLIT, 8, 128)], axis=1
    ).astype(BF16)

    for peer in tensor_peers:
        remote("tensor", peer, send4.at[peer], recv4.at[me_t], 3, rsem4.at[me_t]).start()
    recv4[me_t] = send4[me_t]
    need(get_key, get_value, *get_output)
    score_scale = 1.0 / math.sqrt(HEAD_WIDTH)
    row_of = (iota((32, 1), 0) % 8) // 4
    key_of = iota((32, 1), 0) // 16
    valid = iota((32, SPAN), 1).astype(F32) < jnp.where(row_of == 0, length0, length1)
    self_valid = iota((32, 8), 1) == 4 * row_of

    def eight(t):
        return pl.ds(pl.multiple_of(8 * t, 8), 8)

    def score(plane):
        cols = pl.ds(pl.multiple_of(256 * plane, 256), 256)
        arrived = recv4[pl.ds(4 * plane, 4)].astype(F32)
        q = arrived[:, 0:8, :].reshape(32, 128)
        kv = jnp.sum(arrived[:, 8:16, :].reshape(2, 2, 8, 128), axis=1)
        tail = jnp.concatenate([kv[0], kv[1]], axis=1)
        blocks = jnp.concatenate(
            [jnp.where(key_of == 0, q, 0.0), jnp.where(key_of == 1, q, 0.0)], axis=1
        ).astype(BF16)
        scores = jnp.where(
            row_of == 0,
            dot_tb(blocks, cache_key[0, :, cols]),
            dot_tb(blocks, cache_key[1, :, cols]),
        )
        self_scores = dot_tb(blocks, tail.astype(BF16))
        scores = jnp.where(valid, scores * score_scale, MASKED_SCORE)
        self_scores = jnp.where(self_valid, self_scores * score_scale, MASKED_SCORE)
        return plane, scores, self_scores, pltpu.roll(tail, 7, 0).astype(BF16)

    def attend(plane, scores, self_scores, tail_v):
        cols = pl.ds(pl.multiple_of(256 * plane, 256), 256)
        top = jnp.maximum(
            jnp.max(scores, axis=1, keepdims=True), jnp.max(self_scores, axis=1, keepdims=True)
        )
        weights = jnp.exp(scores - top)
        self_weight = jnp.exp(self_scores - top)
        full_total = jnp.sum(weights, axis=1, keepdims=True) + jnp.sum(
            self_weight, axis=1, keepdims=True
        )
        weights = weights.astype(BF16)
        over = jnp.where(
            row_of == 0,
            dot(weights, cache_value[0, :, cols]),
            dot(weights, cache_value[1, :, cols]),
        ) + dot(self_weight.astype(BF16), tail_v)
        heads = jnp.where(key_of == 0, over[:, 0:128], over[:, 128:256]) / full_total
        send5[pl.ds(pl.multiple_of(32 * plane, 32), 32), :] = heads

    def send_heads(dy):
        for step in TENSOR_STEPS:
            if step[0] == dy:
                peer = tensor_peer(step)
                remote(
                    "tensor", peer, send5.at[eight(peer)], recv5.at[eight(me_t)], 4, rsem5.at[me_t]
                ).start()

    scored = []
    for dy in PLANE_STEPS:
        for dz in (0, 1, 3, 2):
            if dy or dz:
                peer = tensor_peer((dy, dz))
                remote(
                    "tensor", peer, send4.at[peer], recv4.at[peer], 3, rsem4.at[peer]
                ).wait_recv()
        scored.append((dy, score(lax.rem(me_y + dy, 4))))
        if len(scored) > 1:
            done, parts = scored.pop(0)
            attend(*parts)
            send_heads(done)
    for done, parts in scored:
        attend(*parts)
        send_heads(done)
    recv5[eight(me_t), :] = send5[eight(me_t), :]
    sent(0, send1.at[pl.ds(0, GROUPS - 1)])
    sent(1, recv2.at[pl.ds(0, SPLIT - 1)])
    sent(2, send3.at[pl.ds(0, GROUPS - 1)])
    sent(3, send4.at[pl.ds(0, SPLIT - 1)])
    for peer in tensor_peers[::-1]:
        remote(
            "tensor", peer, send5.at[eight(peer)], recv5.at[eight(peer)], 4, rsem5.at[peer]
        ).wait_recv()
    heads = jnp.concatenate(
        [recv5[pl.ds(j, ROWS, stride=4), :].astype(BF16) for j in range(4)], axis=1
    )

    for peer in tensor_peers:
        cols = pl.ds(pl.multiple_of(peer * COLS, COLS), COLS)
        send6[peer] = dot(heads, output_w[:, cols]).astype(BF16)
        remote("tensor", peer, send6.at[peer], recv6.at[me_t], 5, rsem6.at[me_t]).start()
    total = dot(heads, output_w[:, own_cols])
    for dy, dz in TENSOR_STEPS:
        peer = tensor_peer((4 - dy, 4 - dz))
        remote("tensor", peer, send6.at[peer], recv6.at[peer], 5, rsem6.at[peer]).wait_recv()
        total = total + recv6[peer].astype(F32)
    out_ref[...] = total.astype(BF16)
    sent(4, send5.at[pl.ds(0, 8 * (SPLIT - 1))])
    sent(5, send6.at[pl.ds(0, SPLIT - 1)])


def on_device(
    tokens,
    row_adapter_index,
    adapter_store_row,
    lengths,
    query_weight,
    key_weight,
    value_weight,
    output_weight,
    adapter_down_weight,
    adapter_up_query,
    adapter_up_key,
    adapter_up_value,
    cached_key_rows,
    cached_value_rows,
):
    large = pl.BlockSpec(memory_space=pltpu.HBM)
    dma = pltpu.SemaphoreType.DMA
    return pl.pallas_call(
        kernel,
        out_shape=pltpu.VMEM((ROWS, COLS), BF16),
        in_specs=[large] * 14,
        out_specs=pl.BlockSpec(memory_space=pltpu.VMEM),
        scratch_shapes=[
            pltpu.VMEM((1, ROWS), jnp.int32),
            pltpu.VMEM((1, 32), jnp.int32),
            pltpu.VMEM((1, ROWS), jnp.int32),
            pltpu.VMEM((ROWS, COLS), BF16),
            pltpu.VMEM((ROWS, DEPTH), BF16),
            pltpu.VMEM((DEPTH, COLS), BF16),
            pltpu.VMEM((128, DEPTH), BF16),
            pltpu.VMEM((COLS, DEPTH), BF16),
            pltpu.VMEM((256, COLS), BF16),
            pltpu.VMEM((4, 16, COLS), BF16),
            pltpu.VMEM((4, 16, 64), BF16),
            pltpu.VMEM((4, 16, 64), BF16),
            pltpu.VMEM((2, SPAN, 1024), BF16),
            pltpu.VMEM((2, SPAN, 1024), BF16),
            pltpu.VMEM((GROUPS, 16, 384), BF16),
            pltpu.VMEM((GROUPS, 16, 384), BF16),
            pltpu.VMEM((32, 128), BF16),
            pltpu.VMEM((SPLIT, 32, 128), BF16),
            pltpu.VMEM((GROUPS, 16, 384), BF16),
            pltpu.VMEM((GROUPS, 16, 384), BF16),
            pltpu.VMEM((128, 128), F32),
            pltpu.VMEM((128, 128), F32),
            pltpu.VMEM((SPLIT, 16, 128), BF16),
            pltpu.VMEM((SPLIT, 16, 128), BF16),
            pltpu.VMEM((128, 128), F32),
            pltpu.VMEM((128, 128), F32),
            pltpu.VMEM((SPLIT, ROWS, COLS), BF16),
            pltpu.VMEM((SPLIT, ROWS, COLS), BF16),
            dma((20,)),
            dma((QUERY_CHUNKS,)),
            dma((6,)),
            dma((GROUPS,)),
            dma((SPLIT,)),
            dma((GROUPS,)),
            dma((SPLIT,)),
            dma((SPLIT,)),
            dma((SPLIT,)),
        ],
        compiler_params=pltpu.CompilerParams(
            collective_id=0, has_side_effects=True, vmem_limit_bytes=56 * 1024 * 1024
        ),
    )(
        row_adapter_index.reshape(1, ROWS),
        adapter_store_row.reshape(1, 32),
        lengths.reshape(1, ROWS),
        tokens,
        query_weight,
        key_weight.T,
        value_weight.T,
        output_weight,
        adapter_down_weight,
        adapter_up_query,
        adapter_up_key,
        adapter_up_value,
        cached_key_rows,
        cached_value_rows,
    )


def solution(mesh):
    placed = (
        P("batch", None),
        P("batch"),
        P(),
        P("batch"),
        P(None, "tensor"),
        P(None, "tensor"),
        P(None, "tensor"),
        P("tensor", None),
        P("batch", None, "tensor"),
        P("batch", None, "tensor"),
        P("batch", None, "tensor"),
        P("batch", None, "tensor"),
        P(("batch", "tensor"), None, None),
        P(("batch", "tensor"), None, None),
    )
    return jax.shard_map(
        on_device, mesh=mesh, in_specs=placed, out_specs=P("batch", "tensor"), check_vma=False
    )
```

```python
import math

import jax
import jax.numpy as jnp
from jax import lax
from jax.experimental import pallas as pl
from jax.experimental.pallas import tpu as pltpu
from jax.sharding import PartitionSpec as P

HEAD_WIDTH = 128
ADAPTER_SCALE = 0.5
MASKED_SCORE = -1e30
MESH = pl.DeviceIdType.MESH
F32 = jnp.float32
BF16 = jnp.bfloat16

GROUPS = 8
SPLIT = 16
CAP = 8
ROWS = 32
QUERY_CHUNKS = 8
DEPTH = 8192
COLS = 512
SPAN = 512
TRANS_B = (((1,), (1,)), ((), ()))


def iota(shape, dim):
    return lax.broadcasted_iota(jnp.int32, shape, dim)


def dot(a, b):
    return jnp.dot(a, b, preferred_element_type=F32)


def dot_tb(a, b):
    return lax.dot_general(a, b, TRANS_B, preferred_element_type=F32)


def far_first(count):
    steps = [(dy, dz) for dy in range(4) for dz in range(4) if dy or dz]
    return sorted(steps, key=lambda s: -(min(s[0], 4 - s[0]) + min(s[1], 4 - s[1])))


TENSOR_STEPS = far_first(SPLIT)
PLANE_STEPS = (0, 1, 3, 2)
BATCH_STEPS = [(2, 1), (2, 0), (1, 1), (3, 1), (1, 0), (3, 0), (0, 1)]


def kernel(
    index_hbm,
    store_hbm,
    length_hbm,
    tokens_hbm,
    query_hbm,
    key_hbm,
    value_hbm,
    output_hbm,
    down_hbm,
    up_query_hbm,
    up_key_hbm,
    up_value_hbm,
    cache_key_hbm,
    cache_value_hbm,
    out_ref,
    index_ref,
    store_ref,
    length_ref,
    own_tokens,
    tokens,
    query_w,
    kv_w,
    output_w,
    down,
    up_query,
    up_key,
    up_value,
    cache_key,
    cache_value,
    send1,
    recv1,
    send2,
    recv2,
    send3,
    recv3,
    stage_q,
    stage_kv,
    send4,
    recv4,
    send5,
    recv5,
    send6,
    recv6,
    local_sem,
    query_sem,
    plane_sem,
    send_sem,
    rsem1,
    rsem2,
    rsem3,
    rsem4,
    rsem5,
    rsem6,
):
    me_b = lax.axis_index("batch")
    me_t = lax.axis_index("tensor")
    me_x, me_c = me_b // 2, lax.rem(me_b, 2)
    me_y, me_z = me_t // 4, lax.rem(me_t, 4)

    def batch_peer(step):
        core = 1 - me_c if step[1] else me_c
        return lax.rem(me_x + step[0], 4) * 2 + core

    def tensor_peer(step):
        return lax.rem(me_y + step[0], 4) * 4 + lax.rem(me_z + step[1], 4)

    batch_peers = [batch_peer(step) for step in BATCH_STEPS]
    tensor_peers = [tensor_peer(step) for step in TENSOR_STEPS]

    ring_z = [tensor_peer((0, step)) for step in (2, 1, 3)]
    ring_y = [tensor_peer((step, 0)) for step in (2, 1, 3)]

    barrier = pltpu.get_barrier_semaphore()
    for peer in ring_z + ring_y:
        pl.semaphore_signal(barrier, inc=1, device_id={"tensor": peer}, device_id_type=MESH)
    for peer in batch_peers:
        pl.semaphore_signal(barrier, inc=1, device_id={"batch": peer}, device_id_type=MESH)

    pending = []

    def fetch(src, dst, sem):
        copy = pltpu.make_async_copy(src, dst, sem)
        copy.start()
        pending.append(copy)
        return copy

    def need(*copies):
        for copy in copies:
            if any(copy is other for other in pending):
                pending[:] = [other for other in pending if other is not copy]
                copy.wait()

    own_cols = pl.ds(pl.multiple_of(me_t * COLS, COLS), COLS)
    get_index = fetch(index_hbm, index_ref, local_sem.at[0])
    get_store = fetch(store_hbm, store_ref, local_sem.at[1])
    get_own = fetch(tokens_hbm.at[:, own_cols], own_tokens, local_sem.at[2])
    get_down = [
        fetch(down_hbm.at[a], down.at[pl.ds(64 * a, 48), :], local_sem.at[3 + a]) for a in range(4)
    ]
    get_up = [
        fetch(up_query_hbm, up_query, local_sem.at[7]),
        fetch(up_key_hbm, up_key, local_sem.at[8]),
        fetch(up_value_hbm, up_value, local_sem.at[9]),
    ]
    get_length = fetch(length_hbm, length_ref, local_sem.at[10])
    get_tokens = fetch(tokens_hbm, tokens, local_sem.at[11])
    get_kv = [
        fetch(key_hbm, kv_w.at[pl.ds(0, 64), :], local_sem.at[12]),
        fetch(value_hbm, kv_w.at[pl.ds(64, 64), :], local_sem.at[13]),
    ]
    piece = DEPTH // QUERY_CHUNKS
    get_query = [
        fetch(
            query_hbm.at[pl.ds(i * piece, piece), :],
            query_w.at[pl.ds(i * piece, piece), :],
            query_sem.at[i],
        )
        for i in range(QUERY_CHUNKS)
    ]
    get_key = fetch(cache_key_hbm, cache_key, local_sem.at[14])
    get_value = fetch(cache_value_hbm, cache_value, local_sem.at[15])
    get_output = [
        fetch(
            output_hbm.at[pl.ds(i * 128, 128), :],
            output_w.at[pl.ds(i * 128, 128), :],
            local_sem.at[16 + i],
        )
        for i in range(4)
    ]

    row_i = iota((ROWS, ROWS), 0)
    col_i = iota((ROWS, ROWS), 1)
    diag = row_i == col_i
    need(get_index, get_store)
    index_c = jnp.broadcast_to(index_ref[...].astype(F32), (ROWS, ROWS))
    store_c = jnp.broadcast_to(store_ref[...].astype(F32), (ROWS, ROWS))
    index_r = jnp.sum(jnp.where(diag, index_c, 0.0), axis=1, keepdims=True)
    slot_r = jnp.sum(
        jnp.where(index_r == col_i.astype(F32), store_c, 0.0), axis=1, keepdims=True
    )
    slot_c = jnp.sum(jnp.where(diag, slot_r, 0.0), axis=0, keepdims=True)
    owner_r = jnp.floor(slot_r * 0.25)
    owner_c = jnp.floor(slot_c * 0.25)
    within_r = slot_r - 4.0 * owner_r
    same = owner_r == owner_c
    place_c = jnp.sum(jnp.where(same & (row_i < col_i), 1.0, 0.0), axis=0, keepdims=True)
    target_c = owner_c * 16.0 + place_c
    slot_i = iota((128, ROWS), 0)
    route = jnp.where(
        target_c == ((slot_i // 16) * 16 + slot_i % 8).astype(F32), 1.0, 0.0
    ).astype(BF16)
    hot = jnp.where(within_r == iota((ROWS, 128), 1).astype(F32), 1.0, 0.0).astype(BF16)
    lower = (iota((128, 256), 0) % 16) < 8

    need(get_own)
    routed = dot(route, own_tokens[...])
    routed_hot = dot(route, hot)
    send1[:, :, 0:256] = (
        jnp.where(lower, routed[:, 0:256], routed[:, 256:512]).astype(BF16).reshape(GROUPS, 16, 256)
    )
    send1[:, :, 256:384] = routed_hot.astype(BF16).reshape(GROUPS, 16, 128)

    pl.semaphore_wait(barrier, GROUPS - 1 + 6)
    for peer in ring_y:
        pl.semaphore_signal(plane_sem, inc=1, device_id={"tensor": peer}, device_id_type=MESH)

    def remote(axis, peer, source, target, phase, rsem):
        return pltpu.make_async_remote_copy(
            src_ref=source,
            dst_ref=target,
            send_sem=send_sem.at[phase],
            recv_sem=rsem,
            device_id={axis: peer},
            device_id_type=MESH,
        )

    def start_batch(phase, send, recv, rsem):
        for peer in batch_peers:
            remote("batch", peer, send.at[peer], recv.at[me_b], phase, rsem.at[me_b]).start()

    def wait_batch(phase, send, recv, rsem):
        for peer in batch_peers[::-1]:
            remote("batch", peer, send.at[peer], recv.at[peer], phase, rsem.at[peer]).wait_recv()

    def sent(phase, like):
        pltpu.make_async_copy(like, like, send_sem.at[phase]).wait()

    start_batch(0, send1, recv1, rsem1)
    recv1[me_b] = send1[me_b]

    for a in range(4):
        down[pl.ds(64 * a + 48, 16), :] = jnp.zeros((16, COLS), BF16)
    place_r = jnp.sum(jnp.where(same & (col_i < row_i), 1.0, 0.0), axis=1, keepdims=True)
    target_r = owner_r * 16.0 + place_r
    slot_j = iota((ROWS, 128), 1).astype(F32)
    unroute = jnp.concatenate(
        [
            jnp.where(target_r == slot_j, 1.0, 0.0),
            jnp.where(target_r + 8.0 == slot_j, 1.0, 0.0),
        ],
        axis=0,
    ).astype(BF16)
    lane_in = iota((128, 256), 0)
    lane_out = iota((128, 256), 1)
    group_hot = jnp.where(lane_in == lane_out // 64, 1.0, 0.0).astype(BF16)
    turn = jnp.where(lane_out < 64, 16, jnp.where(lane_out < 128, 32, 0))
    wanted = jnp.where(lane_out < 192, turn + lane_out % 16, -256)
    pick = jnp.concatenate(
        [jnp.where(lane_in == wanted, 1.0, 0.0), jnp.where(lane_in == wanted + 64, 1.0, 0.0)],
        axis=1,
    ).astype(BF16)
    spread_hot = jnp.where(lane_in == (lane_out % 64) // 16, 1.0, 0.0).astype(BF16)

    need(get_tokens, *get_kv)
    kv_base = dot_tb(tokens[...], kv_w[...])

    def query_part(total, chunks):
        for i in chunks:
            need(get_query[i])
            total = total + dot(
                tokens[:, i * piece : (i + 1) * piece], query_w[i * piece : (i + 1) * piece, :]
            )
        return total

    q_base = query_part(jnp.zeros((ROWS, COLS), F32), range(0, 3))
    need(*get_down)

    wait_batch(0, send1, recv1, rsem1)
    rows_in = recv1[:, :, 0:256].reshape(128, 256)
    hot_in = recv1[:, :, 256:384].reshape(128, 128)
    empty = jnp.zeros_like(rows_in)
    rows_in = jnp.concatenate(
        [jnp.where(lower, rows_in, empty), jnp.where(lower, empty, rows_in)], axis=1
    )
    shrunk = dot_tb(rows_in, down[...]) * dot(hot_in, group_hot)
    shrunk = shrunk[:, 0:128] + shrunk[:, 128:256]
    shrunk = jnp.sum(shrunk.reshape(GROUPS, 2, CAP, 128), axis=1).reshape(64, 128)
    shrunk = shrunk + pltpu.roll(shrunk, 64, 1)
    send2[...] = jnp.where(iota((32, 128), 1) < 64, shrunk[0:32], shrunk[32:64]).astype(BF16)

    pl.semaphore_wait(plane_sem, 3)
    for peer in tensor_peers:
        remote("tensor", peer, send2, recv2.at[me_t], 1, rsem2.at[me_t]).start()

    hot_rows = dot(hot_in, spread_hot).reshape(GROUPS, 2, CAP, 256)[:, 0].reshape(64, 256)
    need(*get_up)
    up_k = up_key[...].reshape(64, 64)
    up_v = up_value[...].reshape(64, 64)
    blank = jnp.zeros_like(up_k)
    up_kv = jnp.concatenate(
        [jnp.concatenate([up_k, blank], axis=1), jnp.concatenate([blank, up_v], axis=1)], axis=0
    )
    q_base = query_part(q_base, range(3, QUERY_CHUNKS))

    summed = send2[...].astype(F32)
    for peer in tensor_peers[::-1]:
        remote("tensor", peer, send2, recv2.at[peer], 1, rsem2.at[peer]).wait_recv()
        summed = summed + recv2[peer].astype(F32)
    scaled = (ADAPTER_SCALE * summed).astype(BF16)
    spread = dot(scaled, pick)
    spread = jnp.concatenate([spread[:, 0:256], spread[:, 256:512]], axis=0)
    masked = (spread * hot_rows).astype(BF16)
    delta_kv = dot(masked[:, 0:128], up_kv).reshape(GROUPS, CAP, 128)
    delta_q = dot(masked[:, 128:192], up_query[...].reshape(64, COLS)).reshape(GROUPS, CAP, COLS)
    send3[:, :, 0:256] = jnp.concatenate(
        [delta_q[:, :, 0:256], delta_q[:, :, 256:512]], axis=1
    ).astype(BF16)
    send3[:, :, 256:384] = jnp.concatenate([delta_kv, delta_kv], axis=1).astype(BF16)

    start_batch(2, send3, recv3, rsem3)
    recv3[me_b] = send3[me_b]

    parity = lax.rem(me_t, 2)
    half = iota((ROWS, 128), 1) // 64 == parity
    stage_kv[...] = jnp.zeros_like(stage_kv)
    need(get_length)
    length_lane = iota((1, ROWS), 1)
    lengths = length_ref[...].astype(F32)
    length0 = jnp.sum(jnp.where(length_lane == 2 * me_t, lengths, 0.0), axis=1, keepdims=True)
    length1 = jnp.sum(jnp.where(length_lane == 2 * me_t + 1, lengths, 0.0), axis=1, keepdims=True)

    wait_batch(2, send3, recv3, rsem3)
    delta = dot(unroute, recv3[...].reshape(128, 384))
    kv_new = kv_base + delta[0:32, 256:384]
    rolled = pltpu.roll(kv_new, 64, 1)
    k_row = jnp.where(half, jnp.where(parity == 1, rolled, kv_new), 0.0)
    v_row = jnp.where(half, jnp.where(parity == 1, kv_new, rolled), 0.0)
    for j in range(4):
        part = delta[32 * (j // 2) : 32 * (j // 2) + 32, 128 * (j % 2) : 128 * (j % 2) + 128]
        stage_q[pl.ds(j, ROWS, stride=4), :] = q_base[:, 128 * j : 128 * (j + 1)] + part
    stage_kv[pl.ds(0, ROWS, stride=4), :] = k_row
    stage_kv[pl.ds(1, ROWS, stride=4), :] = v_row
    send4[...] = jnp.concatenate(
        [stage_q[...].reshape(SPLIT, 8, 128), stage_kv[...].reshape(SPLIT, 8, 128)], axis=1
    ).astype(BF16)

    for peer in tensor_peers:
        remote("tensor", peer, send4.at[peer], recv4.at[me_t], 3, rsem4.at[me_t]).start()
    recv4[me_t] = send4[me_t]
    need(get_key, get_value, *get_output)
    score_scale = 1.0 / math.sqrt(HEAD_WIDTH)
    row_of = (iota((32, 1), 0) % 8) // 4
    key_of = iota((32, 1), 0) // 16
    valid = iota((32, SPAN), 1).astype(F32) < jnp.where(row_of == 0, length0, length1)
    self_valid = iota((32, 8), 1) == 4 * row_of

    def eight(t):
        return pl.ds(pl.multiple_of(8 * t, 8), 8)

    def score(plane):
        cols = pl.ds(pl.multiple_of(256 * plane, 256), 256)
        arrived = recv4[pl.ds(4 * plane, 4)].astype(F32)
        q = arrived[:, 0:8, :].reshape(32, 128)
        kv = jnp.sum(arrived[:, 8:16, :].reshape(2, 2, 8, 128), axis=1)
        tail = jnp.concatenate([kv[0], kv[1]], axis=1)
        blocks = jnp.concatenate(
            [jnp.where(key_of == 0, q, 0.0), jnp.where(key_of == 1, q, 0.0)], axis=1
        ).astype(BF16)
        scores = jnp.where(
            row_of == 0,
            dot_tb(blocks, cache_key[0, :, cols]),
            dot_tb(blocks, cache_key[1, :, cols]),
        )
        self_scores = dot_tb(blocks, tail.astype(BF16))
        scores = jnp.where(valid, scores * score_scale, MASKED_SCORE)
        self_scores = jnp.where(self_valid, self_scores * score_scale, MASKED_SCORE)
        return plane, scores, self_scores, pltpu.roll(tail, 7, 0).astype(BF16)

    def attend(plane, scores, self_scores, tail_v):
        cols = pl.ds(pl.multiple_of(256 * plane, 256), 256)
        top = jnp.maximum(
            jnp.max(scores, axis=1, keepdims=True), jnp.max(self_scores, axis=1, keepdims=True)
        )
        weights = jnp.exp(scores - top)
        self_weight = jnp.exp(self_scores - top)
        full_total = jnp.sum(weights, axis=1, keepdims=True) + jnp.sum(
            self_weight, axis=1, keepdims=True
        )
        weights = weights.astype(BF16)
        over = jnp.where(
            row_of == 0,
            dot(weights, cache_value[0, :, cols]),
            dot(weights, cache_value[1, :, cols]),
        ) + dot(self_weight.astype(BF16), tail_v)
        heads = jnp.where(key_of == 0, over[:, 0:128], over[:, 128:256]) / full_total
        send5[pl.ds(pl.multiple_of(32 * plane, 32), 32), :] = heads

    def send_heads(dy):
        for step in TENSOR_STEPS:
            if step[0] == dy:
                peer = tensor_peer(step)
                remote(
                    "tensor", peer, send5.at[eight(peer)], recv5.at[eight(me_t)], 4, rsem5.at[me_t]
                ).start()

    scored = []
    for dy in PLANE_STEPS:
        for dz in (0, 1, 3, 2):
            if dy or dz:
                peer = tensor_peer((dy, dz))
                remote(
                    "tensor", peer, send4.at[peer], recv4.at[peer], 3, rsem4.at[peer]
                ).wait_recv()
        scored.append((dy, score(lax.rem(me_y + dy, 4))))
        if len(scored) > 1:
            done, parts = scored.pop(0)
            attend(*parts)
            send_heads(done)
    for done, parts in scored:
        attend(*parts)
        send_heads(done)
    recv5[eight(me_t), :] = send5[eight(me_t), :]
    sent(0, send1.at[pl.ds(0, GROUPS - 1)])
    sent(1, recv2.at[pl.ds(0, SPLIT - 1)])
    sent(2, send3.at[pl.ds(0, GROUPS - 1)])
    sent(3, send4.at[pl.ds(0, SPLIT - 1)])
    for peer in tensor_peers[::-1]:
        remote(
            "tensor", peer, send5.at[eight(peer)], recv5.at[eight(peer)], 4, rsem5.at[peer]
        ).wait_recv()
    heads = jnp.concatenate(
        [recv5[pl.ds(j, ROWS, stride=4), :].astype(BF16) for j in range(4)], axis=1
    )

    for peer in tensor_peers:
        cols = pl.ds(pl.multiple_of(peer * COLS, COLS), COLS)
        send6[peer] = dot(heads, output_w[:, cols]).astype(BF16)
        remote("tensor", peer, send6.at[peer], recv6.at[me_t], 5, rsem6.at[me_t]).start()
    total = dot(heads, output_w[:, own_cols])
    for dy, dz in TENSOR_STEPS:
        peer = tensor_peer((4 - dy, 4 - dz))
        remote("tensor", peer, send6.at[peer], recv6.at[peer], 5, rsem6.at[peer]).wait_recv()
        total = total + recv6[peer].astype(F32)
    out_ref[...] = total.astype(BF16)
    sent(4, send5.at[pl.ds(0, 8 * (SPLIT - 1))])
    sent(5, send6.at[pl.ds(0, SPLIT - 1)])


def on_device(
    tokens,
    row_adapter_index,
    adapter_store_row,
    lengths,
    query_weight,
    key_weight,
    value_weight,
    output_weight,
    adapter_down_weight,
    adapter_up_query,
    adapter_up_key,
    adapter_up_value,
    cached_key_rows,
    cached_value_rows,
):
    large = pl.BlockSpec(memory_space=pltpu.HBM)
    dma = pltpu.SemaphoreType.DMA
    return pl.pallas_call(
        kernel,
        out_shape=pltpu.VMEM((ROWS, COLS), BF16),
        in_specs=[large] * 14,
        out_specs=pl.BlockSpec(memory_space=pltpu.VMEM),
        scratch_shapes=[
            pltpu.VMEM((1, ROWS), jnp.int32),
            pltpu.VMEM((1, 32), jnp.int32),
            pltpu.VMEM((1, ROWS), jnp.int32),
            pltpu.VMEM((ROWS, COLS), BF16),
            pltpu.VMEM((ROWS, DEPTH), BF16),
            pltpu.VMEM((DEPTH, COLS), BF16),
            pltpu.VMEM((128, DEPTH), BF16),
            pltpu.VMEM((COLS, DEPTH), BF16),
            pltpu.VMEM((256, COLS), BF16),
            pltpu.VMEM((4, 16, COLS), BF16),
            pltpu.VMEM((4, 16, 64), BF16),
            pltpu.VMEM((4, 16, 64), BF16),
            pltpu.VMEM((2, SPAN, 1024), BF16),
            pltpu.VMEM((2, SPAN, 1024), BF16),
            pltpu.VMEM((GROUPS, 16, 384), BF16),
            pltpu.VMEM((GROUPS, 16, 384), BF16),
            pltpu.VMEM((32, 128), BF16),
            pltpu.VMEM((SPLIT, 32, 128), BF16),
            pltpu.VMEM((GROUPS, 16, 384), BF16),
            pltpu.VMEM((GROUPS, 16, 384), BF16),
            pltpu.VMEM((128, 128), F32),
            pltpu.VMEM((128, 128), F32),
            pltpu.VMEM((SPLIT, 16, 128), BF16),
            pltpu.VMEM((SPLIT, 16, 128), BF16),
            pltpu.VMEM((128, 128), F32),
            pltpu.VMEM((128, 128), F32),
            pltpu.VMEM((SPLIT, ROWS, COLS), BF16),
            pltpu.VMEM((SPLIT, ROWS, COLS), BF16),
            dma((20,)),
            dma((QUERY_CHUNKS,)),
            pltpu.SemaphoreType.REGULAR,
            dma((6,)),
            dma((GROUPS,)),
            dma((SPLIT,)),
            dma((GROUPS,)),
            dma((SPLIT,)),
            dma((SPLIT,)),
            dma((SPLIT,)),
        ],
        compiler_params=pltpu.CompilerParams(
            collective_id=0, has_side_effects=True, vmem_limit_bytes=56 * 1024 * 1024
        ),
    )(
        row_adapter_index.reshape(1, ROWS),
        adapter_store_row.reshape(1, 32),
        lengths.reshape(1, ROWS),
        tokens,
        query_weight,
        key_weight.T,
        value_weight.T,
        output_weight,
        adapter_down_weight,
        adapter_up_query,
        adapter_up_key,
        adapter_up_value,
        cached_key_rows,
        cached_value_rows,
    )


def solution(mesh):
    placed = (
        P("batch", None),
        P("batch"),
        P(),
        P("batch"),
        P(None, "tensor"),
        P(None, "tensor"),
        P(None, "tensor"),
        P("tensor", None),
        P("batch", None, "tensor"),
        P("batch", None, "tensor"),
        P("batch", None, "tensor"),
        P("batch", None, "tensor"),
        P(("batch", "tensor"), None, None),
        P(("batch", "tensor"), None, None),
    )
    return jax.shard_map(
        on_device, mesh=mesh, in_specs=placed, out_specs=P("batch", "tensor"), check_vma=False
    )
```

```python
import math

import jax
import jax.numpy as jnp
from jax import lax
from jax.experimental import pallas as pl
from jax.experimental.pallas import tpu as pltpu
from jax.sharding import PartitionSpec as P

HEAD_WIDTH = 128
ADAPTER_SCALE = 0.5
MASKED_SCORE = -1e30
MESH = pl.DeviceIdType.MESH
F32 = jnp.float32
BF16 = jnp.bfloat16

GROUPS = 8
SPLIT = 16
CAP = 8
ROWS = 32
QUERY_CHUNKS = 8
DEPTH = 8192
COLS = 512
SPAN = 512
TRANS_B = (((1,), (1,)), ((), ()))


def iota(shape, dim):
    return lax.broadcasted_iota(jnp.int32, shape, dim)


def dot(a, b):
    return jnp.dot(a, b, preferred_element_type=F32)


def dot_tb(a, b):
    return lax.dot_general(a, b, TRANS_B, preferred_element_type=F32)


def far_first(count):
    steps = [(dy, dz) for dy in range(4) for dz in range(4) if dy or dz]
    return sorted(steps, key=lambda s: -(min(s[0], 4 - s[0]) + min(s[1], 4 - s[1])))


TENSOR_STEPS = far_first(SPLIT)
PLANE_STEPS = (0, 3, 1, 2)
BATCH_STEPS = [(2, 1), (2, 0), (1, 1), (3, 1), (1, 0), (3, 0), (0, 1)]


def kernel(
    index_hbm,
    store_hbm,
    length_hbm,
    tokens_hbm,
    query_hbm,
    key_hbm,
    value_hbm,
    output_hbm,
    down_hbm,
    up_query_hbm,
    up_key_hbm,
    up_value_hbm,
    cache_key_hbm,
    cache_value_hbm,
    out_ref,
    index_ref,
    store_ref,
    length_ref,
    own_tokens,
    tokens,
    query_w,
    kv_w,
    output_w,
    down,
    up_query,
    up_key,
    up_value,
    cache_key,
    cache_value,
    send1,
    recv1,
    send2,
    recv2,
    send3,
    recv3,
    stage_q,
    stage_kv,
    send4,
    recv4,
    send5,
    recv5,
    send6,
    recv6,
    local_sem,
    query_sem,
    plane_sem,
    send_sem,
    rsem1,
    rsem2,
    rsem3,
    rsem4,
    rsem5,
    rsem6,
):
    me_b = lax.axis_index("batch")
    me_t = lax.axis_index("tensor")
    me_x, me_c = me_b // 2, lax.rem(me_b, 2)
    me_y, me_z = me_t // 4, lax.rem(me_t, 4)

    def batch_peer(step):
        core = 1 - me_c if step[1] else me_c
        return lax.rem(me_x + step[0], 4) * 2 + core

    def tensor_peer(step):
        return lax.rem(me_y + step[0], 4) * 4 + lax.rem(me_z + step[1], 4)

    batch_peers = [batch_peer(step) for step in BATCH_STEPS]
    tensor_peers = [tensor_peer(step) for step in TENSOR_STEPS]

    ring_z = [tensor_peer((0, step)) for step in (2, 1, 3)]
    ring_y = [tensor_peer((step, 0)) for step in (2, 1, 3)]

    barrier = pltpu.get_barrier_semaphore()
    for peer in batch_peers:
        pl.semaphore_signal(barrier, inc=1, device_id={"batch": peer}, device_id_type=MESH)
    for peer in ring_z + ring_y:
        pl.semaphore_signal(barrier, inc=1, device_id={"tensor": peer}, device_id_type=MESH)

    pending = []

    def fetch(src, dst, sem):
        copy = pltpu.make_async_copy(src, dst, sem)
        copy.start()
        pending.append(copy)
        return copy

    def need(*copies):
        for copy in copies:
            if any(copy is other for other in pending):
                pending[:] = [other for other in pending if other is not copy]
                copy.wait()

    own_cols = pl.ds(pl.multiple_of(me_t * COLS, COLS), COLS)
    get_index = fetch(index_hbm, index_ref, local_sem.at[0])
    get_store = fetch(store_hbm, store_ref, local_sem.at[1])
    get_own = fetch(tokens_hbm.at[:, own_cols], own_tokens, local_sem.at[2])
    get_down = [
        fetch(down_hbm.at[a], down.at[pl.ds(64 * a, 48), :], local_sem.at[3 + a]) for a in range(4)
    ]
    get_up = [
        fetch(up_query_hbm, up_query, local_sem.at[7]),
        fetch(up_key_hbm, up_key, local_sem.at[8]),
        fetch(up_value_hbm, up_value, local_sem.at[9]),
    ]
    get_length = fetch(length_hbm, length_ref, local_sem.at[10])
    get_tokens = fetch(tokens_hbm, tokens, local_sem.at[11])
    get_kv = [
        fetch(key_hbm, kv_w.at[pl.ds(0, 64), :], local_sem.at[12]),
        fetch(value_hbm, kv_w.at[pl.ds(64, 64), :], local_sem.at[13]),
    ]
    piece = DEPTH // QUERY_CHUNKS
    get_query = [
        fetch(
            query_hbm.at[pl.ds(i * piece, piece), :],
            query_w.at[pl.ds(i * piece, piece), :],
            query_sem.at[i],
        )
        for i in range(QUERY_CHUNKS)
    ]
    get_key = fetch(cache_key_hbm, cache_key, local_sem.at[14])
    get_value = fetch(cache_value_hbm, cache_value, local_sem.at[15])
    get_output = [
        fetch(
            output_hbm.at[pl.ds(i * 128, 128), :],
            output_w.at[pl.ds(i * 128, 128), :],
            local_sem.at[16 + i],
        )
        for i in range(4)
    ]

    row_i = iota((ROWS, ROWS), 0)
    col_i = iota((ROWS, ROWS), 1)
    diag = row_i == col_i
    need(get_index, get_store)
    index_c = jnp.broadcast_to(index_ref[...].astype(F32), (ROWS, ROWS))
    store_c = jnp.broadcast_to(store_ref[...].astype(F32), (ROWS, ROWS))
    index_r = jnp.sum(jnp.where(diag, index_c, 0.0), axis=1, keepdims=True)
    slot_r = jnp.sum(
        jnp.where(index_r == col_i.astype(F32), store_c, 0.0), axis=1, keepdims=True
    )
    slot_c = jnp.sum(jnp.where(diag, slot_r, 0.0), axis=0, keepdims=True)
    owner_r = jnp.floor(slot_r * 0.25)
    owner_c = jnp.floor(slot_c * 0.25)
    within_r = slot_r - 4.0 * owner_r
    same = owner_r == owner_c
    place_c = jnp.sum(jnp.where(same & (row_i < col_i), 1.0, 0.0), axis=0, keepdims=True)
    target_c = owner_c * 16.0 + place_c
    slot_i = iota((128, ROWS), 0)
    route = jnp.where(
        target_c == ((slot_i // 16) * 16 + slot_i % 8).astype(F32), 1.0, 0.0
    ).astype(BF16)
    hot = jnp.where(within_r == iota((ROWS, 128), 1).astype(F32), 1.0, 0.0).astype(BF16)
    lower = (iota((128, 256), 0) % 16) < 8

    need(get_own)
    routed = dot(route, own_tokens[...])
    routed_hot = dot(route, hot)
    send1[:, :, 0:256] = (
        jnp.where(lower, routed[:, 0:256], routed[:, 256:512]).astype(BF16).reshape(GROUPS, 16, 256)
    )
    send1[:, :, 256:384] = routed_hot.astype(BF16).reshape(GROUPS, 16, 128)

    pl.semaphore_wait(barrier, GROUPS - 1 + 6)
    for peer in ring_y:
        pl.semaphore_signal(plane_sem, inc=1, device_id={"tensor": peer}, device_id_type=MESH)

    def remote(axis, peer, source, target, phase, rsem):
        return pltpu.make_async_remote_copy(
            src_ref=source,
            dst_ref=target,
            send_sem=send_sem.at[phase],
            recv_sem=rsem,
            device_id={axis: peer},
            device_id_type=MESH,
        )

    def start_batch(phase, send, recv, rsem):
        for peer in batch_peers:
            remote("batch", peer, send.at[peer], recv.at[me_b], phase, rsem.at[me_b]).start()

    def wait_batch(phase, send, recv, rsem):
        for peer in batch_peers[::-1]:
            remote("batch", peer, send.at[peer], recv.at[peer], phase, rsem.at[peer]).wait_recv()

    def sent(phase, like):
        pltpu.make_async_copy(like, like, send_sem.at[phase]).wait()

    start_batch(0, send1, recv1, rsem1)
    recv1[me_b] = send1[me_b]

    for a in range(4):
        down[pl.ds(64 * a + 48, 16), :] = jnp.zeros((16, COLS), BF16)
    place_r = jnp.sum(jnp.where(same & (col_i < row_i), 1.0, 0.0), axis=1, keepdims=True)
    target_r = owner_r * 16.0 + place_r
    slot_j = iota((ROWS, 128), 1).astype(F32)
    unroute = jnp.concatenate(
        [
            jnp.where(target_r == slot_j, 1.0, 0.0),
            jnp.where(target_r + 8.0 == slot_j, 1.0, 0.0),
        ],
        axis=0,
    ).astype(BF16)
    lane_in = iota((128, 256), 0)
    lane_out = iota((128, 256), 1)
    group_hot = jnp.where(lane_in == lane_out // 64, 1.0, 0.0).astype(BF16)
    turn = jnp.where(lane_out < 64, 16, jnp.where(lane_out < 128, 32, 0))
    wanted = jnp.where(lane_out < 192, turn + lane_out % 16, -256)
    pick = jnp.concatenate(
        [jnp.where(lane_in == wanted, 1.0, 0.0), jnp.where(lane_in == wanted + 64, 1.0, 0.0)],
        axis=1,
    ).astype(BF16)
    spread_hot = jnp.where(lane_in == (lane_out % 64) // 16, 1.0, 0.0).astype(BF16)

    need(get_tokens, *get_kv)
    kv_base = dot_tb(tokens[...], kv_w[...])

    def query_part(total, chunks):
        for i in chunks:
            need(get_query[i])
            total = total + dot(
                tokens[:, i * piece : (i + 1) * piece], query_w[i * piece : (i + 1) * piece, :]
            )
        return total

    q_base = query_part(jnp.zeros((ROWS, COLS), F32), range(0, 3))
    need(*get_down)

    wait_batch(0, send1, recv1, rsem1)
    rows_in = recv1[:, :, 0:256].reshape(128, 256)
    hot_in = recv1[:, :, 256:384].reshape(128, 128)
    empty = jnp.zeros_like(rows_in)
    rows_in = jnp.concatenate(
        [jnp.where(lower, rows_in, empty), jnp.where(lower, empty, rows_in)], axis=1
    )
    shrunk = dot_tb(rows_in, down[...]) * dot(hot_in, group_hot)
    shrunk = shrunk[:, 0:128] + shrunk[:, 128:256]
    shrunk = jnp.sum(shrunk.reshape(GROUPS, 2, CAP, 128), axis=1).reshape(64, 128)
    shrunk = shrunk + pltpu.roll(shrunk, 64, 1)
    send2[...] = jnp.where(iota((32, 128), 1) < 64, shrunk[0:32], shrunk[32:64]).astype(BF16)

    pl.semaphore_wait(plane_sem, 3)
    for peer in tensor_peers:
        remote("tensor", peer, send2, recv2.at[me_t], 1, rsem2.at[me_t]).start()

    hot_rows = dot(hot_in, spread_hot).reshape(GROUPS, 2, CAP, 256)[:, 0].reshape(64, 256)
    need(*get_up)
    up_k = up_key[...].reshape(64, 64)
    up_v = up_value[...].reshape(64, 64)
    blank = jnp.zeros_like(up_k)
    up_kv = jnp.concatenate(
        [jnp.concatenate([up_k, blank], axis=1), jnp.concatenate([blank, up_v], axis=1)], axis=0
    )
    q_base = query_part(q_base, range(3, QUERY_CHUNKS))

    summed = send2[...].astype(F32)
    for peer in tensor_peers[::-1]:
        remote("tensor", peer, send2, recv2.at[peer], 1, rsem2.at[peer]).wait_recv()
        summed = summed + recv2[peer].astype(F32)
    scaled = (ADAPTER_SCALE * summed).astype(BF16)
    spread = dot(scaled, pick)
    spread = jnp.concatenate([spread[:, 0:256], spread[:, 256:512]], axis=0)
    masked = (spread * hot_rows).astype(BF16)
    delta_kv = dot(masked[:, 0:128], up_kv).reshape(GROUPS, CAP, 128)
    delta_q = dot(masked[:, 128:192], up_query[...].reshape(64, COLS)).reshape(GROUPS, CAP, COLS)
    send3[:, :, 0:256] = jnp.concatenate(
        [delta_q[:, :, 0:256], delta_q[:, :, 256:512]], axis=1
    ).astype(BF16)
    send3[:, :, 256:384] = jnp.concatenate([delta_kv, delta_kv], axis=1).astype(BF16)

    start_batch(2, send3, recv3, rsem3)
    recv3[me_b] = send3[me_b]

    parity = lax.rem(me_t, 2)
    half = iota((ROWS, 128), 1) // 64 == parity
    stage_kv[...] = jnp.zeros_like(stage_kv)
    need(get_length)
    length_lane = iota((1, ROWS), 1)
    lengths = length_ref[...].astype(F32)
    length0 = jnp.sum(jnp.where(length_lane == 2 * me_t, lengths, 0.0), axis=1, keepdims=True)
    length1 = jnp.sum(jnp.where(length_lane == 2 * me_t + 1, lengths, 0.0), axis=1, keepdims=True)

    wait_batch(2, send3, recv3, rsem3)
    delta = dot(unroute, recv3[...].reshape(128, 384))
    kv_new = kv_base + delta[0:32, 256:384]
    rolled = pltpu.roll(kv_new, 64, 1)
    k_row = jnp.where(half, jnp.where(parity == 1, rolled, kv_new), 0.0)
    v_row = jnp.where(half, jnp.where(parity == 1, kv_new, rolled), 0.0)
    for j in range(4):
        part = delta[32 * (j // 2) : 32 * (j // 2) + 32, 128 * (j % 2) : 128 * (j % 2) + 128]
        stage_q[pl.ds(j, ROWS, stride=4), :] = q_base[:, 128 * j : 128 * (j + 1)] + part
    stage_kv[pl.ds(0, ROWS, stride=4), :] = k_row
    stage_kv[pl.ds(1, ROWS, stride=4), :] = v_row
    send4[...] = jnp.concatenate(
        [stage_q[...].reshape(SPLIT, 8, 128), stage_kv[...].reshape(SPLIT, 8, 128)], axis=1
    ).astype(BF16)

    for peer in tensor_peers:
        remote("tensor", peer, send4.at[peer], recv4.at[me_t], 3, rsem4.at[me_t]).start()
    recv4[me_t] = send4[me_t]
    need(get_key, get_value, *get_output)
    score_scale = 1.0 / math.sqrt(HEAD_WIDTH)
    row_of = (iota((32, 1), 0) % 8) // 4
    key_of = iota((32, 1), 0) // 16
    valid = iota((32, SPAN), 1).astype(F32) < jnp.where(row_of == 0, length0, length1)
    self_valid = iota((32, 8), 1) == 4 * row_of

    def eight(t):
        return pl.ds(pl.multiple_of(8 * t, 8), 8)

    def score(plane):
        cols = pl.ds(pl.multiple_of(256 * plane, 256), 256)
        arrived = recv4[pl.ds(4 * plane, 4)].astype(F32)
        q = arrived[:, 0:8, :].reshape(32, 128)
        kv = jnp.sum(arrived[:, 8:16, :].reshape(2, 2, 8, 128), axis=1)
        tail = jnp.concatenate([kv[0], kv[1]], axis=1)
        blocks = jnp.concatenate(
            [jnp.where(key_of == 0, q, 0.0), jnp.where(key_of == 1, q, 0.0)], axis=1
        ).astype(BF16)
        scores = jnp.where(
            row_of == 0,
            dot_tb(blocks, cache_key[0, :, cols]),
            dot_tb(blocks, cache_key[1, :, cols]),
        )
        self_scores = dot_tb(blocks, tail.astype(BF16))
        scores = jnp.where(valid, scores * score_scale, MASKED_SCORE)
        self_scores = jnp.where(self_valid, self_scores * score_scale, MASKED_SCORE)
        return plane, scores, self_scores, pltpu.roll(tail, 7, 0).astype(BF16)

    def attend(plane, scores, self_scores, tail_v):
        cols = pl.ds(pl.multiple_of(256 * plane, 256), 256)
        top = jnp.maximum(
            jnp.max(scores, axis=1, keepdims=True), jnp.max(self_scores, axis=1, keepdims=True)
        )
        weights = jnp.exp(scores - top)
        self_weight = jnp.exp(self_scores - top)
        full_total = jnp.sum(weights, axis=1, keepdims=True) + jnp.sum(
            self_weight, axis=1, keepdims=True
        )
        weights = weights.astype(BF16)
        over = jnp.where(
            row_of == 0,
            dot(weights, cache_value[0, :, cols]),
            dot(weights, cache_value[1, :, cols]),
        ) + dot(self_weight.astype(BF16), tail_v)
        heads = jnp.where(key_of == 0, over[:, 0:128], over[:, 128:256]) / full_total
        send5[pl.ds(pl.multiple_of(32 * plane, 32), 32), :] = heads

    def send_heads(dy):
        for step in TENSOR_STEPS:
            if step[0] == dy:
                peer = tensor_peer(step)
                remote(
                    "tensor", peer, send5.at[eight(peer)], recv5.at[eight(me_t)], 4, rsem5.at[me_t]
                ).start()

    scored = []
    for dy in PLANE_STEPS:
        for dz in (0, 1, 3, 2):
            if dy or dz:
                peer = tensor_peer((dy, dz))
                remote(
                    "tensor", peer, send4.at[peer], recv4.at[peer], 3, rsem4.at[peer]
                ).wait_recv()
        scored.append((dy, score(lax.rem(me_y + dy, 4))))
        if len(scored) > 1:
            done, parts = scored.pop(0)
            attend(*parts)
            send_heads(done)
    for done, parts in scored:
        attend(*parts)
        send_heads(done)
    recv5[eight(me_t), :] = send5[eight(me_t), :]
    sent(0, send1.at[pl.ds(0, GROUPS - 1)])
    sent(1, recv2.at[pl.ds(0, SPLIT - 1)])
    sent(2, send3.at[pl.ds(0, GROUPS - 1)])
    sent(3, send4.at[pl.ds(0, SPLIT - 1)])
    for peer in tensor_peers[::-1]:
        remote(
            "tensor", peer, send5.at[eight(peer)], recv5.at[eight(peer)], 4, rsem5.at[peer]
        ).wait_recv()
    heads = jnp.concatenate(
        [recv5[pl.ds(j, ROWS, stride=4), :].astype(BF16) for j in range(4)], axis=1
    )

    for peer in tensor_peers:
        cols = pl.ds(pl.multiple_of(peer * COLS, COLS), COLS)
        send6[peer] = dot(heads, output_w[:, cols]).astype(BF16)
        remote("tensor", peer, send6.at[peer], recv6.at[me_t], 5, rsem6.at[me_t]).start()
    total = dot(heads, output_w[:, own_cols])
    for dy, dz in TENSOR_STEPS:
        peer = tensor_peer((4 - dy, 4 - dz))
        remote("tensor", peer, send6.at[peer], recv6.at[peer], 5, rsem6.at[peer]).wait_recv()
        total = total + recv6[peer].astype(F32)
    out_ref[...] = total.astype(BF16)
    sent(4, send5.at[pl.ds(0, 8 * (SPLIT - 1))])
    sent(5, send6.at[pl.ds(0, SPLIT - 1)])


def on_device(
    tokens,
    row_adapter_index,
    adapter_store_row,
    lengths,
    query_weight,
    key_weight,
    value_weight,
    output_weight,
    adapter_down_weight,
    adapter_up_query,
    adapter_up_key,
    adapter_up_value,
    cached_key_rows,
    cached_value_rows,
):
    large = pl.BlockSpec(memory_space=pltpu.HBM)
    dma = pltpu.SemaphoreType.DMA
    return pl.pallas_call(
        kernel,
        out_shape=pltpu.VMEM((ROWS, COLS), BF16),
        in_specs=[large] * 14,
        out_specs=pl.BlockSpec(memory_space=pltpu.VMEM),
        scratch_shapes=[
            pltpu.VMEM((1, ROWS), jnp.int32),
            pltpu.VMEM((1, 32), jnp.int32),
            pltpu.VMEM((1, ROWS), jnp.int32),
            pltpu.VMEM((ROWS, COLS), BF16),
            pltpu.VMEM((ROWS, DEPTH), BF16),
            pltpu.VMEM((DEPTH, COLS), BF16),
            pltpu.VMEM((128, DEPTH), BF16),
            pltpu.VMEM((COLS, DEPTH), BF16),
            pltpu.VMEM((256, COLS), BF16),
            pltpu.VMEM((4, 16, COLS), BF16),
            pltpu.VMEM((4, 16, 64), BF16),
            pltpu.VMEM((4, 16, 64), BF16),
            pltpu.VMEM((2, SPAN, 1024), BF16),
            pltpu.VMEM((2, SPAN, 1024), BF16),
            pltpu.VMEM((GROUPS, 16, 384), BF16),
            pltpu.VMEM((GROUPS, 16, 384), BF16),
            pltpu.VMEM((32, 128), BF16),
            pltpu.VMEM((SPLIT, 32, 128), BF16),
            pltpu.VMEM((GROUPS, 16, 384), BF16),
            pltpu.VMEM((GROUPS, 16, 384), BF16),
            pltpu.VMEM((128, 128), F32),
            pltpu.VMEM((128, 128), F32),
            pltpu.VMEM((SPLIT, 16, 128), BF16),
            pltpu.VMEM((SPLIT, 16, 128), BF16),
            pltpu.VMEM((128, 128), F32),
            pltpu.VMEM((128, 128), F32),
            pltpu.VMEM((SPLIT, ROWS, COLS), BF16),
            pltpu.VMEM((SPLIT, ROWS, COLS), BF16),
            dma((20,)),
            dma((QUERY_CHUNKS,)),
            pltpu.SemaphoreType.REGULAR,
            dma((6,)),
            dma((GROUPS,)),
            dma((SPLIT,)),
            dma((GROUPS,)),
            dma((SPLIT,)),
            dma((SPLIT,)),
            dma((SPLIT,)),
        ],
        compiler_params=pltpu.CompilerParams(
            collective_id=0, has_side_effects=True, vmem_limit_bytes=56 * 1024 * 1024
        ),
    )(
        row_adapter_index.reshape(1, ROWS),
        adapter_store_row.reshape(1, 32),
        lengths.reshape(1, ROWS),
        tokens,
        query_weight,
        key_weight.T,
        value_weight.T,
        output_weight,
        adapter_down_weight,
        adapter_up_query,
        adapter_up_key,
        adapter_up_value,
        cached_key_rows,
        cached_value_rows,
    )


def solution(mesh):
    placed = (
        P("batch", None),
        P("batch"),
        P(),
        P("batch"),
        P(None, "tensor"),
        P(None, "tensor"),
        P(None, "tensor"),
        P("tensor", None),
        P("batch", None, "tensor"),
        P("batch", None, "tensor"),
        P("batch", None, "tensor"),
        P("batch", None, "tensor"),
        P(("batch", "tensor"), None, None),
        P(("batch", "tensor"), None, None),
    )
    return jax.shard_map(
        on_device, mesh=mesh, in_specs=placed, out_specs=P("batch", "tensor"), check_vma=False
    )
```

```python
import math

import jax
import jax.numpy as jnp
from jax import lax
from jax.experimental import pallas as pl
from jax.experimental.pallas import tpu as pltpu
from jax.sharding import PartitionSpec as P

HEAD_WIDTH = 128
ADAPTER_SCALE = 0.5
MASKED_SCORE = -1e30
MESH = pl.DeviceIdType.MESH
F32 = jnp.float32
BF16 = jnp.bfloat16

GROUPS = 8
SPLIT = 16
CAP = 8
ROWS = 32
QUERY_CHUNKS = 8
DEPTH = 8192
COLS = 512
SPAN = 512
TRANS_B = (((1,), (1,)), ((), ()))


def iota(shape, dim):
    return lax.broadcasted_iota(jnp.int32, shape, dim)


def dot(a, b):
    return jnp.dot(a, b, preferred_element_type=F32)


def dot_tb(a, b):
    return lax.dot_general(a, b, TRANS_B, preferred_element_type=F32)


def far_first(count):
    steps = [(dy, dz) for dy in range(4) for dz in range(4) if dy or dz]
    return sorted(steps, key=lambda s: -(min(s[0], 4 - s[0]) + min(s[1], 4 - s[1])))


TENSOR_STEPS = far_first(SPLIT)
PLANE_STEPS = (0, 3, 1, 2)
BATCH_STEPS = [(2, 1), (2, 0), (1, 1), (3, 1), (1, 0), (3, 0), (0, 1)]


def kernel(
    index_hbm,
    store_hbm,
    length_hbm,
    tokens_hbm,
    query_hbm,
    key_hbm,
    value_hbm,
    output_hbm,
    down_hbm,
    up_query_hbm,
    up_key_hbm,
    up_value_hbm,
    cache_key_hbm,
    cache_value_hbm,
    out_ref,
    index_ref,
    store_ref,
    length_ref,
    own_tokens,
    tokens,
    query_w,
    kv_w,
    output_w,
    down,
    up_query,
    up_key,
    up_value,
    cache_key,
    cache_value,
    send1,
    recv1,
    send2,
    recv2,
    send3,
    recv3,
    stage_q,
    stage_kv,
    send4,
    recv4,
    send5,
    recv5,
    send6,
    recv6,
    local_sem,
    query_sem,
    plane_sem,
    send_sem,
    rsem1,
    rsem2,
    rsem3,
    rsem4,
    rsem5,
    rsem6,
):
    me_b = lax.axis_index("batch")
    me_t = lax.axis_index("tensor")
    me_x, me_c = me_b // 2, lax.rem(me_b, 2)
    me_y, me_z = me_t // 4, lax.rem(me_t, 4)

    def batch_peer(step):
        core = 1 - me_c if step[1] else me_c
        return lax.rem(me_x + step[0], 4) * 2 + core

    def tensor_peer(step):
        return lax.rem(me_y + step[0], 4) * 4 + lax.rem(me_z + step[1], 4)

    batch_peers = [batch_peer(step) for step in BATCH_STEPS]
    tensor_peers = [tensor_peer(step) for step in TENSOR_STEPS]

    ring_z = [tensor_peer((0, step)) for step in (2, 1, 3)]
    ring_y = [tensor_peer((step, 0)) for step in (2, 1, 3)]

    barrier = pltpu.get_barrier_semaphore()
    for peer in batch_peers:
        pl.semaphore_signal(barrier, inc=1, device_id={"batch": peer}, device_id_type=MESH)
    for peer in ring_z + ring_y:
        pl.semaphore_signal(barrier, inc=1, device_id={"tensor": peer}, device_id_type=MESH)

    pending = []

    def fetch(src, dst, sem):
        copy = pltpu.make_async_copy(src, dst, sem)
        copy.start()
        pending.append(copy)
        return copy

    def need(*copies):
        for copy in copies:
            if any(copy is other for other in pending):
                pending[:] = [other for other in pending if other is not copy]
                copy.wait()

    own_cols = pl.ds(pl.multiple_of(me_t * COLS, COLS), COLS)
    get_index = fetch(index_hbm, index_ref, local_sem.at[0])
    get_store = fetch(store_hbm, store_ref, local_sem.at[1])
    get_own = fetch(tokens_hbm.at[:, own_cols], own_tokens, local_sem.at[2])
    get_down = [
        fetch(down_hbm.at[a], down.at[pl.ds(64 * a, 48), :], local_sem.at[3 + a]) for a in range(4)
    ]
    get_up = [
        fetch(up_query_hbm, up_query, local_sem.at[7]),
        fetch(up_key_hbm, up_key, local_sem.at[8]),
        fetch(up_value_hbm, up_value, local_sem.at[9]),
    ]
    get_length = fetch(length_hbm, length_ref, local_sem.at[10])
    get_tokens = fetch(tokens_hbm, tokens, local_sem.at[11])
    get_kv = [
        fetch(key_hbm, kv_w.at[pl.ds(0, 64), :], local_sem.at[12]),
        fetch(value_hbm, kv_w.at[pl.ds(64, 64), :], local_sem.at[13]),
    ]
    piece = DEPTH // QUERY_CHUNKS
    get_query = [
        fetch(
            query_hbm.at[pl.ds(i * piece, piece), :],
            query_w.at[pl.ds(i * piece, piece), :],
            query_sem.at[i],
        )
        for i in range(QUERY_CHUNKS)
    ]
    get_key = fetch(cache_key_hbm, cache_key, local_sem.at[14])
    get_value = fetch(cache_value_hbm, cache_value, local_sem.at[15])
    get_output = [
        fetch(
            output_hbm.at[pl.ds(i * 128, 128), :],
            output_w.at[pl.ds(i * 128, 128), :],
            local_sem.at[16 + i],
        )
        for i in range(4)
    ]

    row_i = iota((ROWS, ROWS), 0)
    col_i = iota((ROWS, ROWS), 1)
    diag = row_i == col_i
    need(get_index, get_store)
    index_c = jnp.broadcast_to(index_ref[...].astype(F32), (ROWS, ROWS))
    store_c = jnp.broadcast_to(store_ref[...].astype(F32), (ROWS, ROWS))
    index_r = jnp.sum(jnp.where(diag, index_c, 0.0), axis=1, keepdims=True)
    slot_r = jnp.sum(
        jnp.where(index_r == col_i.astype(F32), store_c, 0.0), axis=1, keepdims=True
    )
    slot_c = jnp.sum(jnp.where(diag, slot_r, 0.0), axis=0, keepdims=True)
    owner_r = jnp.floor(slot_r * 0.25)
    owner_c = jnp.floor(slot_c * 0.25)
    within_r = slot_r - 4.0 * owner_r
    same = owner_r == owner_c
    place_c = jnp.sum(jnp.where(same & (row_i < col_i), 1.0, 0.0), axis=0, keepdims=True)
    target_c = owner_c * 16.0 + place_c
    slot_i = iota((128, ROWS), 0)
    route = jnp.where(
        target_c == ((slot_i // 16) * 16 + slot_i % 8).astype(F32), 1.0, 0.0
    ).astype(BF16)
    hot = jnp.where(within_r == iota((ROWS, 128), 1).astype(F32), 1.0, 0.0).astype(BF16)
    lower = (iota((128, 256), 0) % 16) < 8

    need(get_own)
    routed = dot(route, own_tokens[...])
    routed_hot = dot(route, hot)
    send1[:, :, 0:256] = (
        jnp.where(lower, routed[:, 0:256], routed[:, 256:512]).astype(BF16).reshape(GROUPS, 16, 256)
    )
    send1[:, :, 256:384] = routed_hot.astype(BF16).reshape(GROUPS, 16, 128)

    pl.semaphore_wait(barrier, GROUPS - 1 + 6)
    for peer in ring_y:
        pl.semaphore_signal(plane_sem, inc=1, device_id={"tensor": peer}, device_id_type=MESH)

    def remote(axis, peer, source, target, phase, rsem):
        return pltpu.make_async_remote_copy(
            src_ref=source,
            dst_ref=target,
            send_sem=send_sem.at[phase],
            recv_sem=rsem,
            device_id={axis: peer},
            device_id_type=MESH,
        )

    def start_batch(phase, send, recv, rsem):
        for peer in batch_peers:
            remote("batch", peer, send.at[peer], recv.at[me_b], phase, rsem.at[me_b]).start()

    def wait_batch(phase, send, recv, rsem):
        for peer in batch_peers[::-1]:
            remote("batch", peer, send.at[peer], recv.at[peer], phase, rsem.at[peer]).wait_recv()

    def sent(phase, like):
        pltpu.make_async_copy(like, like, send_sem.at[phase]).wait()

    start_batch(0, send1, recv1, rsem1)
    recv1[me_b] = send1[me_b]

    for a in range(4):
        down[pl.ds(64 * a + 48, 16), :] = jnp.zeros((16, COLS), BF16)
    place_r = jnp.sum(jnp.where(same & (col_i < row_i), 1.0, 0.0), axis=1, keepdims=True)
    target_r = owner_r * 16.0 + place_r
    slot_j = iota((ROWS, 128), 1).astype(F32)
    unroute = jnp.concatenate(
        [
            jnp.where(target_r == slot_j, 1.0, 0.0),
            jnp.where(target_r + 8.0 == slot_j, 1.0, 0.0),
        ],
        axis=0,
    ).astype(BF16)
    lane_in = iota((128, 256), 0)
    lane_out = iota((128, 256), 1)
    group_hot = jnp.where(lane_in == lane_out // 64, 1.0, 0.0).astype(BF16)
    turn = jnp.where(lane_out < 64, 16, jnp.where(lane_out < 128, 32, 0))
    wanted = jnp.where(lane_out < 192, turn + lane_out % 16, -256)
    pick = jnp.concatenate(
        [jnp.where(lane_in == wanted, 1.0, 0.0), jnp.where(lane_in == wanted + 64, 1.0, 0.0)],
        axis=1,
    ).astype(BF16)
    spread_hot = jnp.where(lane_in == (lane_out % 64) // 16, 1.0, 0.0).astype(BF16)

    need(get_tokens, *get_kv)
    kv_base = dot_tb(tokens[...], kv_w[...])

    def query_part(total, chunks):
        for i in chunks:
            need(get_query[i])
            total = total + dot(
                tokens[:, i * piece : (i + 1) * piece], query_w[i * piece : (i + 1) * piece, :]
            )
        return total

    q_base = query_part(jnp.zeros((ROWS, COLS), F32), range(0, 3))
    need(*get_down)

    wait_batch(0, send1, recv1, rsem1)
    rows_in = recv1[:, :, 0:256].reshape(128, 256)
    hot_in = recv1[:, :, 256:384].reshape(128, 128)
    empty = jnp.zeros_like(rows_in)
    rows_in = jnp.concatenate(
        [jnp.where(lower, rows_in, empty), jnp.where(lower, empty, rows_in)], axis=1
    )
    shrunk = dot_tb(rows_in, down[...]) * dot(hot_in, group_hot)
    shrunk = shrunk[:, 0:128] + shrunk[:, 128:256]
    shrunk = jnp.sum(shrunk.reshape(GROUPS, 2, CAP, 128), axis=1).reshape(64, 128)
    shrunk = shrunk + pltpu.roll(shrunk, 64, 1)
    send2[...] = jnp.where(iota((32, 128), 1) < 64, shrunk[0:32], shrunk[32:64]).astype(BF16)

    pl.semaphore_wait(plane_sem, 3)
    for peer in tensor_peers:
        remote("tensor", peer, send2, recv2.at[me_t], 1, rsem2.at[me_t]).start()

    hot_rows = dot(hot_in, spread_hot).reshape(GROUPS, 2, CAP, 256)[:, 0].reshape(64, 256)
    need(*get_up)
    up_k = up_key[...].reshape(64, 64)
    up_v = up_value[...].reshape(64, 64)
    blank = jnp.zeros_like(up_k)
    up_kv = jnp.concatenate(
        [jnp.concatenate([up_k, blank], axis=1), jnp.concatenate([blank, up_v], axis=1)], axis=0
    )
    q_base = query_part(q_base, range(3, QUERY_CHUNKS))

    summed = send2[...].astype(F32)
    for peer in tensor_peers[::-1]:
        remote("tensor", peer, send2, recv2.at[peer], 1, rsem2.at[peer]).wait_recv()
        summed = summed + recv2[peer].astype(F32)
    scaled = (ADAPTER_SCALE * summed).astype(BF16)
    spread = dot(scaled, pick)
    spread = jnp.concatenate([spread[:, 0:256], spread[:, 256:512]], axis=0)
    masked = (spread * hot_rows).astype(BF16)
    delta_kv = dot(masked[:, 0:128], up_kv).reshape(GROUPS, CAP, 128)
    delta_q = dot(masked[:, 128:192], up_query[...].reshape(64, COLS)).reshape(GROUPS, CAP, COLS)
    send3[:, :, 0:256] = jnp.concatenate(
        [delta_q[:, :, 0:256], delta_q[:, :, 256:512]], axis=1
    ).astype(BF16)
    send3[:, :, 256:384] = jnp.concatenate([delta_kv, delta_kv], axis=1).astype(BF16)

    start_batch(2, send3, recv3, rsem3)
    recv3[me_b] = send3[me_b]

    parity = lax.rem(me_t, 2)
    half = iota((ROWS, 128), 1) // 64 == parity
    stage_kv[...] = jnp.zeros_like(stage_kv)
    need(get_length)
    length_lane = iota((1, ROWS), 1)
    lengths = length_ref[...].astype(F32)
    length0 = jnp.sum(jnp.where(length_lane == 2 * me_t, lengths, 0.0), axis=1, keepdims=True)
    length1 = jnp.sum(jnp.where(length_lane == 2 * me_t + 1, lengths, 0.0), axis=1, keepdims=True)

    wait_batch(2, send3, recv3, rsem3)
    delta = dot(unroute, recv3[...].reshape(128, 384))
    kv_new = kv_base + delta[0:32, 256:384]
    rolled = pltpu.roll(kv_new, 64, 1)
    k_row = jnp.where(half, jnp.where(parity == 1, rolled, kv_new), 0.0)
    v_row = jnp.where(half, jnp.where(parity == 1, kv_new, rolled), 0.0)
    for j in range(4):
        part = delta[32 * (j // 2) : 32 * (j // 2) + 32, 128 * (j % 2) : 128 * (j % 2) + 128]
        stage_q[pl.ds(j, ROWS, stride=4), :] = q_base[:, 128 * j : 128 * (j + 1)] + part
    stage_kv[pl.ds(0, ROWS, stride=4), :] = k_row
    stage_kv[pl.ds(1, ROWS, stride=4), :] = v_row
    send4[...] = jnp.concatenate(
        [stage_q[...].reshape(SPLIT, 8, 128), stage_kv[...].reshape(SPLIT, 8, 128)], axis=1
    ).astype(BF16)

    for peer in tensor_peers:
        remote("tensor", peer, send4.at[peer], recv4.at[me_t], 3, rsem4.at[me_t]).start()
    recv4[me_t] = send4[me_t]
    need(get_key, get_value, *get_output)
    score_scale = 1.0 / math.sqrt(HEAD_WIDTH)
    row_of = (iota((32, 1), 0) % 8) // 4
    key_of = iota((32, 1), 0) // 16
    valid = iota((32, SPAN), 1).astype(F32) < jnp.where(row_of == 0, length0, length1)
    self_valid = iota((32, 8), 1) == 4 * row_of

    def eight(t):
        return pl.ds(pl.multiple_of(8 * t, 8), 8)

    def score(plane):
        cols = pl.ds(pl.multiple_of(256 * plane, 256), 256)
        arrived = recv4[pl.ds(4 * plane, 4)].astype(F32)
        q = arrived[:, 0:8, :].reshape(32, 128)
        kv = jnp.sum(arrived[:, 8:16, :].reshape(2, 2, 8, 128), axis=1)
        tail = jnp.concatenate([kv[0], kv[1]], axis=1)
        blocks = jnp.concatenate(
            [jnp.where(key_of == 0, q, 0.0), jnp.where(key_of == 1, q, 0.0)], axis=1
        ).astype(BF16)
        scores = jnp.where(
            row_of == 0,
            dot_tb(blocks, cache_key[0, :, cols]),
            dot_tb(blocks, cache_key[1, :, cols]),
        )
        self_scores = dot_tb(blocks, tail.astype(BF16))
        scores = jnp.where(valid, scores * score_scale, MASKED_SCORE)
        self_scores = jnp.where(self_valid, self_scores * score_scale, MASKED_SCORE)
        return plane, scores, self_scores, pltpu.roll(tail, 7, 0).astype(BF16)

    def attend(plane, scores, self_scores, tail_v):
        cols = pl.ds(pl.multiple_of(256 * plane, 256), 256)
        top = jnp.maximum(
            jnp.max(scores, axis=1, keepdims=True), jnp.max(self_scores, axis=1, keepdims=True)
        )
        weights = jnp.exp(scores - top)
        self_weight = jnp.exp(self_scores - top)
        full_total = jnp.sum(weights, axis=1, keepdims=True) + jnp.sum(
            self_weight, axis=1, keepdims=True
        )
        weights = weights.astype(BF16)
        over = jnp.where(
            row_of == 0,
            dot(weights, cache_value[0, :, cols]),
            dot(weights, cache_value[1, :, cols]),
        ) + dot(self_weight.astype(BF16), tail_v)
        heads = jnp.where(key_of == 0, over[:, 0:128], over[:, 128:256]) / full_total
        send5[pl.ds(pl.multiple_of(32 * plane, 32), 32), :] = heads

    def send_heads(dy):
        for step in TENSOR_STEPS:
            if step[0] == dy:
                peer = tensor_peer(step)
                remote(
                    "tensor", peer, send5.at[eight(peer)], recv5.at[eight(me_t)], 4, rsem5.at[me_t]
                ).start()

    scored = []
    for dy in PLANE_STEPS:
        for dz in (0, 1, 3, 2):
            if dy or dz:
                peer = tensor_peer((dy, dz))
                remote(
                    "tensor", peer, send4.at[peer], recv4.at[peer], 3, rsem4.at[peer]
                ).wait_recv()
        scored.append((dy, score(lax.rem(me_y + dy, 4))))
        if len(scored) > 1:
            done, parts = scored.pop(0)
            attend(*parts)
            send_heads(done)
    for done, parts in scored:
        attend(*parts)
        send_heads(done)
    recv5[eight(me_t), :] = send5[eight(me_t), :]
    sent(0, send1.at[pl.ds(0, GROUPS - 1)])
    sent(1, recv2.at[pl.ds(0, SPLIT - 1)])
    sent(2, send3.at[pl.ds(0, GROUPS - 1)])
    sent(3, send4.at[pl.ds(0, SPLIT - 1)])
    for peer in tensor_peers[::-1]:
        remote(
            "tensor", peer, send5.at[eight(peer)], recv5.at[eight(peer)], 4, rsem5.at[peer]
        ).wait_recv()
    heads = jnp.concatenate(
        [recv5[pl.ds(j, ROWS, stride=4), :].astype(BF16) for j in range(4)], axis=1
    )

    sum_steps = [(1, 2), (3, 2), (0, 2), (2, 2), (2, 1), (2, 3), (2, 0), (1, 1), (3, 3), (1, 3), (3, 1), (1, 0), (3, 0), (0, 1), (0, 3)]
    for peer in [tensor_peer(step) for step in sum_steps]:
        cols = pl.ds(pl.multiple_of(peer * COLS, COLS), COLS)
        send6[peer] = dot(heads, output_w[:, cols]).astype(BF16)
        remote("tensor", peer, send6.at[peer], recv6.at[me_t], 5, rsem6.at[me_t]).start()
    total = dot(heads, output_w[:, own_cols])
    for dy, dz in sum_steps:
        peer = tensor_peer((4 - dy, 4 - dz))
        remote("tensor", peer, send6.at[peer], recv6.at[peer], 5, rsem6.at[peer]).wait_recv()
        total = total + recv6[peer].astype(F32)
    out_ref[...] = total.astype(BF16)
    sent(4, send5.at[pl.ds(0, 8 * (SPLIT - 1))])
    sent(5, send6.at[pl.ds(0, SPLIT - 1)])


def on_device(
    tokens,
    row_adapter_index,
    adapter_store_row,
    lengths,
    query_weight,
    key_weight,
    value_weight,
    output_weight,
    adapter_down_weight,
    adapter_up_query,
    adapter_up_key,
    adapter_up_value,
    cached_key_rows,
    cached_value_rows,
):
    large = pl.BlockSpec(memory_space=pltpu.HBM)
    dma = pltpu.SemaphoreType.DMA
    return pl.pallas_call(
        kernel,
        out_shape=pltpu.VMEM((ROWS, COLS), BF16),
        in_specs=[large] * 14,
        out_specs=pl.BlockSpec(memory_space=pltpu.VMEM),
        scratch_shapes=[
            pltpu.VMEM((1, ROWS), jnp.int32),
            pltpu.VMEM((1, 32), jnp.int32),
            pltpu.VMEM((1, ROWS), jnp.int32),
            pltpu.VMEM((ROWS, COLS), BF16),
            pltpu.VMEM((ROWS, DEPTH), BF16),
            pltpu.VMEM((DEPTH, COLS), BF16),
            pltpu.VMEM((128, DEPTH), BF16),
            pltpu.VMEM((COLS, DEPTH), BF16),
            pltpu.VMEM((256, COLS), BF16),
            pltpu.VMEM((4, 16, COLS), BF16),
            pltpu.VMEM((4, 16, 64), BF16),
            pltpu.VMEM((4, 16, 64), BF16),
            pltpu.VMEM((2, SPAN, 1024), BF16),
            pltpu.VMEM((2, SPAN, 1024), BF16),
            pltpu.VMEM((GROUPS, 16, 384), BF16),
            pltpu.VMEM((GROUPS, 16, 384), BF16),
            pltpu.VMEM((32, 128), BF16),
            pltpu.VMEM((SPLIT, 32, 128), BF16),
            pltpu.VMEM((GROUPS, 16, 384), BF16),
            pltpu.VMEM((GROUPS, 16, 384), BF16),
            pltpu.VMEM((128, 128), F32),
            pltpu.VMEM((128, 128), F32),
            pltpu.VMEM((SPLIT, 16, 128), BF16),
            pltpu.VMEM((SPLIT, 16, 128), BF16),
            pltpu.VMEM((128, 128), F32),
            pltpu.VMEM((128, 128), F32),
            pltpu.VMEM((SPLIT, ROWS, COLS), BF16),
            pltpu.VMEM((SPLIT, ROWS, COLS), BF16),
            dma((20,)),
            dma((QUERY_CHUNKS,)),
            pltpu.SemaphoreType.REGULAR,
            dma((6,)),
            dma((GROUPS,)),
            dma((SPLIT,)),
            dma((GROUPS,)),
            dma((SPLIT,)),
            dma((SPLIT,)),
            dma((SPLIT,)),
        ],
        compiler_params=pltpu.CompilerParams(
            collective_id=0, has_side_effects=True, vmem_limit_bytes=56 * 1024 * 1024
        ),
    )(
        row_adapter_index.reshape(1, ROWS),
        adapter_store_row.reshape(1, 32),
        lengths.reshape(1, ROWS),
        tokens,
        query_weight,
        key_weight.T,
        value_weight.T,
        output_weight,
        adapter_down_weight,
        adapter_up_query,
        adapter_up_key,
        adapter_up_value,
        cached_key_rows,
        cached_value_rows,
    )


def solution(mesh):
    placed = (
        P("batch", None),
        P("batch"),
        P(),
        P("batch"),
        P(None, "tensor"),
        P(None, "tensor"),
        P(None, "tensor"),
        P("tensor", None),
        P("batch", None, "tensor"),
        P("batch", None, "tensor"),
        P("batch", None, "tensor"),
        P("batch", None, "tensor"),
        P(("batch", "tensor"), None, None),
        P(("batch", "tensor"), None, None),
    )
    return jax.shard_map(
        on_device, mesh=mesh, in_specs=placed, out_specs=P("batch", "tensor"), check_vma=False
    )
```
